32 devices in a mesh: slab: 4 (over y, x), chan: 8 (over z, core).
Axes of the slice: x: 2, y: 2, z: 4, core: 2. Of those that a mesh axis runs over, the one named last changes fastest.
Arguments:
- voltages: bfloat16 [64, 2, 188, 6144], P('chan', None, None, 'slab'), may hold values from -120 to 120
- steering: float32 [64, 2, 64, 188], P('chan'), may hold values from -0.6 to 0.6
- beam_index: int32 [36], replicated, may hold values from 0 to 63
- channel_flags: int32 [64], replicated, may hold values 0 or 1
Outputs:
- beam_output: bfloat16 [64, 2, 36, 6144], P('chan', None, None, 'slab')
The draws below stay inside these ranges and needn't reach their ends.
All inputs are finite; a program needn't handle non-finite values.
Results may differ from the reference program's by a relative error of at most 0.0065.
Values may be sent and summed in bfloat16 or wider, within the bound.
No kernel may reach another device: no remote copies, remote signals or barrier semaphores. Data moves between devices by JAX's collectives and lax.ppermute only.
A program may use at most 128 MiB of HBM per device.

```python
import math
import jax
import jax.numpy as jnp
from jax import lax

P_SIZE = 188
BEAMS = 36
NDIR = 64
HW = 8
CHANNELS = 64
TIME = 6144


def draw_voltages(key, part):
    key = jax.random.fold_in(key, 17)
    scale_key, gain_key, body_key = jax.random.split(key, 3)
    spread = math.log(10.0)
    port_scale = jnp.exp(jax.random.uniform(scale_key, (P_SIZE,), jnp.float32, 0.0, spread))
    channel_gain = jnp.exp(jax.random.uniform(gain_key, (CHANNELS,), jnp.float32, -0.7, 0.7))

    def one_channel(channel):
        subkeys = jax.random.split(jax.random.fold_in(body_key, channel), 4)
        noise_part = jnp.clip(jax.random.normal(subkeys[0], (2, P_SIZE, TIME), jnp.float32), -5.0, 5.0)
        rolled = jnp.roll(noise_part, 1, axis=1)
        real_part = noise_part[0] + 0.5 * rolled[0] - 0.4 * rolled[1]
        imag_part = noise_part[1] + 0.5 * rolled[1] + 0.4 * rolled[0]
        port_gains = 0.3 * jax.random.normal(subkeys[1], (4, 2, P_SIZE), jnp.float32)
        signal = jnp.clip(jax.random.normal(subkeys[2], (4, 2, TIME), jnp.float32), -4.0, 4.0)
        levels = jnp.exp(jax.random.uniform(subkeys[3], (4, TIME // 64 + 1), jnp.float32, math.log(0.3), math.log(3.0)))
        envelope = jnp.repeat(levels, 64, axis=1)[:, :TIME]
        amplitude = signal * envelope[:, None, :]
        for source in range(4):
            real_part = real_part + port_gains[source, 0][:, None] * amplitude[source, 0][None, :] - port_gains[source, 1][:, None] * amplitude[source, 1][None, :]
            imag_part = imag_part + port_gains[source, 0][:, None] * amplitude[source, 1][None, :] + port_gains[source, 1][:, None] * amplitude[source, 0][None, :]
        stacked_parts = jnp.stack([real_part, imag_part], 0) * port_scale[None, :, None] * channel_gain[channel]
        return jnp.clip(stacked_parts, -120.0, 120.0)
    result = lax.map(one_channel, jnp.arange(CHANNELS, dtype=jnp.int32))
    return result.astype(jnp.bfloat16)


def with_ends(array, rng, low, high):
    longest = array.shape.index(max(array.shape))
    spots = []
    for shift in (0, 1):
        where = [jax.random.randint(jax.random.fold_in(rng, axis), (), 0, length) for axis, length in enumerate(array.shape)]
        where[longest] = (where[longest] + shift) % array.shape[longest]
        spots.append(tuple(where))
    return array.at[spots[0]].set(low).at[spots[1]].set(high)


def block_scale(own_key, extent, cuts, least, top_value):
    gain = 1.0
    for dim, shards_of in cuts:
        heights = jax.random.uniform(jax.random.fold_in(jax.random.fold_in(own_key, 6), dim), (shards_of,), jnp.float32, least / len(cuts), top_value / len(cuts))
        gain = gain * jnp.repeat(jnp.exp(heights), extent[dim] // shards_of).reshape((-1,) + (1,) * (len(extent) - 1 - dim))
    return gain


def noise(rng, dims, width, limit, cuts=(), kind=jnp.bfloat16):
    factor_of = block_scale(rng, dims, cuts, -0.22, 0.18) if cuts else 1.0
    array = jax.random.normal(rng, dims, jnp.float32) * width * factor_of
    return jnp.minimum(jnp.maximum(array, -limit), limit).astype(kind)


def setup_inputs(seed: int = 0) -> dict:
    arg_keys = jax.random.split(jax.random.key(seed), 5)
    voltages = draw_voltages(jax.random.fold_in(arg_keys[4], 71), 0)
    steering = noise(arg_keys[1], (CHANNELS, 2, NDIR, P_SIZE), 0.1, 0.6, ((0, 8),), jnp.float32)
    beam_index = with_ends(jax.random.randint(arg_keys[2], (BEAMS,), 0, NDIR), jax.random.fold_in(arg_keys[2], 1), 0, NDIR - 1).astype(jnp.int32)
    channel_flags = with_ends((jax.random.randint(arg_keys[3], (CHANNELS,), 0, 4) < 3).astype(jnp.int32), jax.random.fold_in(arg_keys[3], 1), 0, 1)
    return dict(voltages=voltages, steering=steering, beam_index=beam_index, channel_flags=channel_flags)


LOADING = 0.1

def solve_one(acm_one, steer_one, selector, flag_one):
    port_count = acm_one.shape[-1]
    q_real = acm_one[0]
    q_imag = acm_one[1]
    loading = LOADING * jnp.trace(q_real) / port_count
    q_real = q_real + loading * jnp.eye(port_count, dtype=q_real.dtype)
    real_form = jnp.concatenate([jnp.concatenate([q_real, -q_imag], 1), jnp.concatenate([q_imag, q_real], 1)], 0)
    chosen = jnp.einsum('bn,knp->kbp', selector, steer_one, precision=lax.Precision.HIGHEST)
    targets = jnp.concatenate([chosen[0].T, chosen[1].T], 0)
    factor = jnp.linalg.cholesky(real_form)
    halfway = jax.scipy.linalg.solve_triangular(factor, targets, lower=True)
    solution = jax.scipy.linalg.solve_triangular(factor, halfway, lower=True, trans=1)
    denominator = jnp.sum(targets * solution, axis=0)
    scaled = solution * (flag_one / denominator)[None, :]
    return jnp.stack([scaled[:port_count].T, scaled[port_count:].T], 0).astype(jnp.bfloat16)

def reference(voltages, steering, beam_index, channel_flags):
    stacked = voltages.reshape(CHANNELS, 2 * P_SIZE, TIME)

    def gram_one(block):
        gram_matrix = jnp.dot(block.astype(jnp.float32), block.T.astype(jnp.float32), preferred_element_type=jnp.float32)
        real_part = gram_matrix[:P_SIZE, :P_SIZE] + gram_matrix[P_SIZE:, P_SIZE:]
        imag_part = gram_matrix[P_SIZE:, :P_SIZE] - gram_matrix[:P_SIZE, P_SIZE:]
        return jnp.stack([real_part, imag_part], 0)
    acm = lax.map(gram_one, stacked)
    flag_values = channel_flags.astype(jnp.float32)
    masked = acm * flag_values[:, None, None, None]
    padded = jnp.pad(masked, ((HW, HW), (0, 0), (0, 0), (0, 0)))
    smoothed = (1.0 - flag_values)[:, None, None, None] * acm
    for offset in range(2 * HW + 1):
        smoothed = smoothed + padded[offset:offset + CHANNELS]
    directions = jnp.arange(NDIR, dtype=jnp.int32)
    selector = (beam_index[:, None] == directions[None, :]).astype(jnp.float32)

    def solve_items(items):
        return solve_one(items[0], items[1], selector, items[2])
    weights = lax.map(solve_items, (smoothed, steering, flag_values))

    def beam_one(items):
        weight_one, block = items
        w_real = weight_one[0]
        w_imag = weight_one[1]
        stacked_weights = jnp.concatenate([jnp.concatenate([w_real, w_imag], 1), jnp.concatenate([-w_imag, w_real], 1)], 0)
        product = jnp.dot(stacked_weights.astype(jnp.float32), block.astype(jnp.float32), preferred_element_type=jnp.float32)
        return product.reshape(2, BEAMS, TIME).astype(jnp.bfloat16)
    return lax.map(beam_one, (weights, stacked))
```

```python
import functools

import jax
import jax.numpy as jnp
from jax import lax
from jax.experimental import pallas as pl
from jax.experimental.pallas import tpu as pltpu
from jax.sharding import PartitionSpec as P

HW = 8


LOADING = 0.1

LANES = 128
VMEM_LIMIT = 48 * 1024 * 1024
SQUARINGS = 8


def round_up(value, multiple):
    return -(-value // multiple) * multiple


def dot_nn(left, right):
    return lax.dot_general(
        left, right, (((1,), (0,)), ((), ())), preferred_element_type=jnp.float32
    )


def dot_nt(left, right):
    return lax.dot_general(
        left, right, (((1,), (1,)), ((), ())), preferred_element_type=jnp.float32
    )


def iotas(rows, cols):
    return (
        lax.broadcasted_iota(jnp.int32, (rows, cols), 0),
        lax.broadcasted_iota(jnp.int32, (rows, cols), 1),
    )


def fold(square):
    half = square.shape[0] // 2
    rest = square[:, LANES:]
    return jnp.concatenate(
        [square[:, :LANES], jnp.concatenate([rest[:half], rest[half:]], axis=1)], axis=0
    )


def unfold(folded):
    size = folded.shape[0] * 2 // 3
    width = size - LANES
    rest = jnp.concatenate([folded[size:, :width], folded[size:, width:]], axis=0)
    return jnp.concatenate([folded[:size], rest], axis=1)


def split(x):
    high = x.astype(jnp.bfloat16)
    return high, (x - high.astype(jnp.float32)).astype(jnp.bfloat16)


def covariance_kernel(first_ref, flags_ref, volt_ref, up_ref, down_ref, own_ref, kept):
    step = pl.program_id(0)
    channels, size = kept.shape[0], kept.shape[1] * 2 // 3
    volt = volt_ref[0].astype(jnp.float32)
    blank = jnp.zeros((size - volt.shape[0], volt.shape[2]), jnp.float32)
    v_real = jnp.concatenate([volt[:, 0, :], blank], 0).astype(jnp.bfloat16)
    v_imag = jnp.concatenate([volt[:, 1, :], blank], 0).astype(jnp.bfloat16)
    real_part = dot_nt(v_real, v_real) + dot_nt(v_imag, v_imag)
    cross = dot_nt(v_imag, v_real)
    row, col = iotas(size, size)
    kept[step] = fold(jnp.where(row >= col, real_part, cross - cross.T))

    @pl.when(step == pl.num_programs(0) - 1)
    def _():
        flags = [flags_ref[first_ref[0] + c].astype(jnp.float32) for c in range(channels)]
        for start in range(0, kept.shape[1], 16):
            part = slice(start, start + 16)
            plain = [kept[c, part] for c in range(channels)]
            masked = [plain[c] * flags[c] for c in range(channels)]
            total = masked[0]
            down_ref[0, part] = total.astype(down_ref.dtype)
            for c in range(1, channels):
                total = total + masked[c]
                down_ref[c, part] = total.astype(down_ref.dtype)
            for c in range(channels):
                own_ref[c, part] = total + (1.0 - flags[c]) * plain[c]
            total = masked[-1]
            up_ref[channels - 1, part] = total.astype(up_ref.dtype)
            for c in range(channels - 2, -1, -1):
                total = total + masked[c]
                up_ref[c, part] = total.astype(up_ref.dtype)


def covariances(first, flags, voltages, size):
    channels, _, ports, samples = voltages.shape
    folded = (channels, size + size // 2, LANES)
    whole = pl.BlockSpec(folded, lambda i, *_: (0, 0, 0))
    return pl.pallas_call(
        covariance_kernel,
        grid_spec=pltpu.PrefetchScalarGridSpec(
            num_scalar_prefetch=2,
            grid=(channels,),
            in_specs=[pl.BlockSpec((1, ports, 2, samples), lambda i, *_: (i, 0, 0, 0))],
            out_specs=[whole, whole, whole],
            scratch_shapes=[pltpu.VMEM(folded, jnp.float32)],
        ),
        out_shape=[
            jax.ShapeDtypeStruct(folded, jnp.bfloat16),
            jax.ShapeDtypeStruct(folded, jnp.bfloat16),
            jax.ShapeDtypeStruct(folded, jnp.float32),
        ],
        compiler_params=pltpu.CompilerParams(vmem_limit_bytes=VMEM_LIMIT),
    )(first, flags, jnp.transpose(voltages, (0, 2, 1, 3)))


def window_kernel(slab_ref, own_ref, before_ref, after_ref, mine_ref, *sent_refs):
    share = mine_ref.shape[0]

    def window(slab):
        rows = pl.ds(slab * share, share)
        ends = before_ref[rows].astype(jnp.float32) + after_ref[rows].astype(jnp.float32)
        return own_ref[rows] + ends

    mine_ref[...] = window(slab_ref[0])
    for turn, sent_ref in enumerate(sent_refs, 1):
        sent_ref[...] = window(slab_ref[0] ^ turn).astype(sent_ref.dtype)


def windows(slab, own, before, after, slabs):
    shape = (own.shape[0] // slabs,) + own.shape[1:]
    return pl.pallas_call(
        window_kernel,
        in_specs=[pl.BlockSpec(memory_space=pltpu.SMEM)]
        + [pl.BlockSpec(own.shape, lambda: (0, 0, 0))] * 3,
        out_specs=[pl.BlockSpec(shape, lambda: (0, 0, 0))] * slabs,
        out_shape=[jax.ShapeDtypeStruct(shape, jnp.float32)]
        + [jax.ShapeDtypeStruct(shape, jnp.bfloat16)] * (slabs - 1),
        compiler_params=pltpu.CompilerParams(vmem_limit_bytes=VMEM_LIMIT),
    )(slab, own, before, after)


def choose_kernel(slab_ref, index_ref, steer_ref, out_ref):
    beams, half = index_ref.shape[0], out_ref.shape[1] // 2
    ports = steer_ref.shape[3]
    out_ref[...] = jnp.zeros_like(out_ref)
    for channel in range(out_ref.shape[0]):
        for part in range(2):
            for beam in range(beams):
                row = steer_ref[channel, part, pl.ds(index_ref[beam], 1), :]
                out_ref[channel, pl.ds(part * half + beam, 1), pl.ds(0, ports)] = row


def chosen_vectors(slab, beam_index, steering, share, half, size):
    directions, ports = steering.shape[2:]
    return pl.pallas_call(
        choose_kernel,
        grid_spec=pltpu.PrefetchScalarGridSpec(
            num_scalar_prefetch=2,
            grid=(1,),
            in_specs=[
                pl.BlockSpec((share, 2, directions, ports), lambda i, slab, _: (slab[0], 0, 0, 0))
            ],
            out_specs=pl.BlockSpec((share, 2 * half, size), lambda i, *_: (0, 0, 0)),
        ),
        out_shape=jax.ShapeDtypeStruct((share, 2 * half, size), jnp.float32),
        compiler_params=pltpu.CompilerParams(vmem_limit_bytes=VMEM_LIMIT),
    )(slab, beam_index, steering)


def gains(bound, steps):
    spread, out = (bound - 1.0) / (bound + 1.0), []
    for _ in range(steps):
        centre = spread * spread / 2
        out.append(1.0 / (1.0 - centre))
        spread = centre / (1.0 - centre)
    return out


def solve_kernel(ports, beams, first_ref, flags_ref, *refs):
    own_ref, *got_refs, chosen_ref, weight_ref = refs
    share, half, size = weight_ref.shape[0], chosen_ref.shape[1] // 2, chosen_ref.shape[2]
    bound = ports / LOADING + 1.0
    row, col = iotas(size, size)
    diagonal = row == col
    channels = range(share)
    state = []
    for c in channels:
        folded = own_ref[c]
        for got_ref in got_refs:
            folded = folded + got_ref[c].astype(jnp.float32)
        packed = unfold(folded)
        turned = packed.T
        on_diagonal = jnp.where(diagonal, packed, 0.0)
        trace = jnp.sum(jnp.sum(on_diagonal, axis=0, keepdims=True), axis=1, keepdims=True)
        loading = trace * (LOADING / ports)
        scale = 2.0 / (loading * (1.0 + bound))
        real_part = jnp.where(row >= col, packed, turned)
        real_part = real_part + jnp.where(diagonal & (row < ports), loading, 0.0)
        imag_part = jnp.where(diagonal, 0.0, jnp.where(row < col, packed, -turned))
        state.append((real_part * scale, imag_part * scale, chosen_ref[c] * scale))
    steps = gains(bound, SQUARINGS)
    for number, gain in enumerate(steps):
        squares = number + 1 < len(steps)
        for c in channels:
            real, imag, y = state[c]
            (rh, rl), (ih, il), (yh, yl) = split(real), split(imag), split(y)
            stack = functools.partial(jnp.concatenate, axis=0)
            if squares:
                by_rh = dot_nn(stack([yh, yl, rh, rl]), rh)
                by_rl = dot_nn(stack([yh, rh]), rl)
                by_ih = dot_nn(stack([yh, yl, ih, il, rh, rl]), ih)
                by_il = dot_nn(stack([yh, ih, rh]), il)
            else:
                by_rh, by_rl = dot_nn(stack([yh, yl]), rh), dot_nn(yh, rl)
                by_ih, by_il = dot_nn(stack([yh, yl]), ih), dot_nn(yh, il)
            n = 2 * half
            with_real = by_rh[:n] + by_rh[n : 2 * n] + by_rl[:n]
            with_imag = by_ih[:n] + by_ih[n : 2 * n] + by_il[:n]
            product = stack(
                [with_real[:half] + with_imag[half:], with_real[half:] - with_imag[:half]]
            )
            y = gain * (2.0 * y - product)
            if squares:
                m = size
                rr = by_rh[2 * n : 2 * n + m] + by_rh[2 * n + m :] + by_rl[n:]
                ii = by_ih[2 * n : 2 * n + m] + by_ih[2 * n + m : 2 * n + 2 * m] + by_il[n : n + m]
                ri = by_ih[2 * n + 2 * m : 2 * n + 3 * m] + by_ih[2 * n + 3 * m :] + by_il[n + m :]
                real = gain * (2.0 * real - (rr - ii))
                imag = gain * (2.0 * imag - (ri - ri.T))
            state[c] = real, imag, y
    beam = lax.broadcasted_iota(jnp.int32, (half, 1), 0)
    for c in channels:
        y = state[c][2]
        sums = jnp.sum(y * chosen_ref[c], axis=1, keepdims=True)
        denominator = jnp.where(beam < beams, sums[:half] + sums[half:], 1.0)
        flag = flags_ref[first_ref[0] + c].astype(jnp.float32)
        factor = jnp.where(beam < beams, flag / denominator, 0.0)
        weights = y * jnp.concatenate([factor, factor], axis=0)
        low = weights[:, :LANES]
        high = weights[:, LANES:]
        weight_ref[c, : 2 * half] = low.astype(jnp.bfloat16)
        weight_ref[c, 2 * half :] = jnp.concatenate([high[:half], high[half:]], axis=1).astype(
            jnp.bfloat16
        )


def solved_weights(first, flags, own, got, chosen, ports, beams):
    share, rows, _ = chosen.shape
    smem = pl.BlockSpec(memory_space=pltpu.SMEM)
    whole = [pl.BlockSpec(a.shape, lambda: (0, 0, 0)) for a in (own, *got, chosen)]
    shape = (share, rows + rows // 2, LANES)
    return pl.pallas_call(
        functools.partial(solve_kernel, ports, beams),
        in_specs=[smem, smem] + whole,
        out_specs=pl.BlockSpec(shape, lambda: (0, 0, 0)),
        out_shape=jax.ShapeDtypeStruct(shape, jnp.bfloat16),
        compiler_params=pltpu.CompilerParams(vmem_limit_bytes=VMEM_LIMIT),
    )(first, flags, own, *got, chosen)


def one_hot(rows, cols, hits):
    row, col = iotas(rows, cols)
    table = jnp.zeros((rows, cols), jnp.float32)
    for parity, target, sign in hits:
        hit = (row % 2 == parity) & (col == row // 2 + target)
        table = jnp.where(hit, sign, table)
    return table.astype(jnp.bfloat16)


def beam_kernel(slab_ref, volt_ref, *refs):
    *weight_refs, out_ref = refs
    share, rows, _ = weight_refs[0].shape
    half = rows // 3
    ports, samples = volt_ref.shape[1], volt_ref.shape[3]
    beams = out_ref.shape[1]
    step = pl.program_id(0)
    turn, place = step // share, step % share
    folded = weight_refs[0][place].astype(jnp.float32)
    for number, weight_ref in enumerate(weight_refs[1:], 1):
        folded = jnp.where(turn == number, weight_ref[place].astype(jnp.float32), folded)
    width = (ports - LANES + 63) // 64 * 64
    rest = folded[2 * half :]
    rest = jnp.concatenate([rest[:, :width], rest[:, width : 2 * width]], axis=0)
    weights = jnp.concatenate([folded[: 2 * half], rest], axis=1).astype(jnp.bfloat16)
    size = weights.shape[1]
    to_even = one_hot(2 * beams, 2 * half, [(0, 0, 1.0), (1, half, -1.0)])
    to_odd = one_hot(2 * beams, 2 * half, [(0, half, 1.0), (1, 0, 1.0)])
    even = dot_nn(to_even, weights).astype(jnp.bfloat16)
    odd = dot_nn(to_odd, weights).astype(jnp.bfloat16)
    row, col = iotas(size, 2 * ports)
    spread_even = (col == 2 * row).astype(jnp.float32).astype(jnp.bfloat16)
    spread_odd = (col == 2 * row + 1).astype(jnp.float32).astype(jnp.bfloat16)
    mixed = (dot_nn(even, spread_even) + dot_nn(odd, spread_odd)).astype(jnp.bfloat16)
    formed = dot_nn(mixed, volt_ref[0].reshape(2 * ports, samples))
    out_ref[0] = formed.astype(jnp.bfloat16).reshape(beams, 2, samples)


def formed_beams(slab, voltages, weights, beams):
    channels, _, ports, samples = voltages.shape
    share = weights[0].shape[0]

    def place(i, slab):
        return ((slab[0] ^ (i // share)) * share + i % share, 0, 0, 0)

    out = pl.pallas_call(
        beam_kernel,
        grid_spec=pltpu.PrefetchScalarGridSpec(
            num_scalar_prefetch=1,
            grid=(channels,),
            in_specs=[pl.BlockSpec((1, ports, 2, samples), place)]
            + [pl.BlockSpec(w.shape, lambda i, _: (0, 0, 0)) for w in weights],
            out_specs=pl.BlockSpec((1, beams, 2, samples), place),
        ),
        out_shape=jax.ShapeDtypeStruct((channels, beams, 2, samples), jnp.bfloat16),
        compiler_params=pltpu.CompilerParams(vmem_limit_bytes=VMEM_LIMIT),
    )(slab, jnp.transpose(voltages, (0, 2, 1, 3)), *weights)
    return jnp.transpose(out, (0, 2, 1, 3))


def body(voltages, steering, beam_index, channel_flags):
    channel_count, _, port_count, _ = voltages.shape
    beam_count = beam_index.shape[0]
    slabs, blocks = lax.axis_size("slab"), lax.axis_size("chan")
    if channel_count != HW or slabs & (slabs - 1):
        raise ValueError("unsupported mesh")
    share = channel_count // slabs
    size = round_up(port_count, 64)
    half = round_up(beam_count, 8)
    slab = lax.axis_index("slab").astype(jnp.int32).reshape(1)
    first_channel = (lax.axis_index("chan") * channel_count).astype(jnp.int32).reshape(1)
    chosen = chosen_vectors(slab, beam_index, steering, share, half, size)
    from_here, up_to_here, own = covariances(first_channel, channel_flags, voltages, size)
    upward = [(i, i + 1) for i in range(blocks - 1)]
    before = lax.ppermute(from_here, "chan", upward)
    after = lax.ppermute(up_to_here, "chan", [(j, i) for i, j in upward])
    mine, *sent = windows(slab, own, before, after, slabs)

    def swap(arrays):
        return [
            lax.ppermute(array, "slab", [(i, i ^ turn) for i in range(slabs)])
            for turn, array in enumerate(arrays, 1)
        ]

    got = swap(sent)
    first_share = first_channel + slab * share
    weights = solved_weights(first_share, channel_flags, mine, got, chosen, port_count, beam_count)
    others = swap([weights] * (slabs - 1))
    return formed_beams(slab, voltages, [weights, *others], beam_count)


def solution(mesh):
    return jax.shard_map(
        body,
        mesh=mesh,
        in_specs=(P("chan", None, None, "slab"), P("chan", None, None, None), P(), P()),
        out_specs=P("chan", None, None, "slab"),
        check_vma=False,
    )
```

```python
import functools

import jax
import jax.numpy as jnp
from jax import lax
from jax.experimental import pallas as pl
from jax.experimental.pallas import tpu as pltpu
from jax.sharding import PartitionSpec as P

HW = 8


LOADING = 0.1

LANES = 128
VMEM_LIMIT = 24 * 1024 * 1024
SQUARINGS = 8


def round_up(value, multiple):
    return -(-value // multiple) * multiple


def dot_nn(left, right):
    return lax.dot_general(
        left, right, (((1,), (0,)), ((), ())), preferred_element_type=jnp.float32
    )


def dot_nt(left, right):
    return lax.dot_general(
        left, right, (((1,), (1,)), ((), ())), preferred_element_type=jnp.float32
    )


def iotas(rows, cols):
    return (
        lax.broadcasted_iota(jnp.int32, (rows, cols), 0),
        lax.broadcasted_iota(jnp.int32, (rows, cols), 1),
    )


def unfold(folded):
    size = folded.shape[0] * 2 // 3
    width = LANES // 2
    rest = jnp.concatenate([folded[size:, :width], folded[size:, width:]], axis=0)
    return jnp.concatenate([folded[:size], rest], axis=1)


def split(x):
    high = x.astype(jnp.bfloat16)
    return high, (x - high.astype(jnp.float32)).astype(jnp.bfloat16)


def combine(even_rows, odd_rows):
    lane = lax.broadcasted_iota(jnp.int32, even_rows.shape, 1)
    real = even_rows + pltpu.roll(odd_rows, LANES - 1, 1)
    return jnp.where(lane % 2 == 0, real, pltpu.roll(odd_rows, 1, 1) - even_rows)


def gram(volt, left_ref, right_ref):
    lead = left_ref.shape[1] // 2
    rest = volt.shape[0] - lead
    left, right = dot_nt(volt, volt[:lead]), dot_nt(volt[lead:], volt[lead:])
    left_ref[0, : volt.shape[0]] = left[:, :LANES]
    left_ref[1, : volt.shape[0], : lead - LANES] = left[:, LANES:]
    right_ref[0, :rest] = right[:, :LANES]
    right_ref[1, :rest, : rest - LANES] = right[:, LANES:]


def pack(left_ref, right_ref, out_ref):
    half = left_ref.shape[1] // 4

    def rows(ref, lanes, first, parity):
        return ref[lanes, pl.ds(2 * first + parity, half, stride=2), :]

    top = []
    for lanes in range(2):
        row, lane = iotas(half, LANES)
        gap = lane + lanes * LANES - 2 * row
        first = [rows(left_ref, lanes, 0, parity) for parity in range(2)]
        second = [rows(right_ref, lanes, 0, parity) for parity in range(2)]
        even = jnp.where(gap <= 0, first[0], jnp.where(gap == 1, -second[1], second[0]))
        odd = jnp.where(gap == 0, second[0], jnp.where(gap <= 1, first[1], second[1]))
        top.append((even, odd))
    low = [[rows(left_ref, lanes, half, parity) for parity in range(2)] for lanes in range(2)]
    width = LANES // 2
    side = [
        jnp.concatenate([above[:, :width], below[:, :width]], axis=1)
        for above, below in zip(top[1], low[1])
    ]
    for place, pair in enumerate((top[0], low[0], side)):
        out_ref[place * half : (place + 1) * half] = combine(*pair)


def covariance_kernel(
    first_ref, flags_ref, volt_hbm, across_ref, inside_ref, own_ref, volts, lefts, rights, kept, sems
):
    channels, ports, _, samples = volts.shape
    copies = [
        pltpu.make_async_copy(volt_hbm.at[c], volts.at[c], sems.at[c]) for c in range(channels)
    ]
    groups = [range(c, c + 2) for c in range(0, channels, 2)]
    for group in groups[:2]:
        for c in group:
            copies[c].start()
    lefts[...] = jnp.zeros_like(lefts)
    rights[...] = jnp.zeros_like(rights)
    for number, group in enumerate(groups):
        for c in group:
            copies[c].wait()
        for later in groups[number + 2 : number + 3]:
            for c in later:
                copies[c].start()
        for c in group:
            gram(volts[c].reshape(2 * ports, samples), lefts.at[c], rights.at[c])
        for c in groups[number - 1] if number else ():
            pack(lefts.at[c], rights.at[c], kept.at[c])
    for c in groups[-1]:
        pack(lefts.at[c], rights.at[c], kept.at[c])
    flags = [flags_ref[first_ref[0] + c].astype(jnp.float32) for c in range(channels)]
    odd_block = (first_ref[0] // channels) % 2 == 1
    for start in range(0, kept.shape[1], 16):
        part = slice(start, start + 16)
        plain = [kept[c, part] for c in range(channels)]
        masked = [plain[c] * flags[c] for c in range(channels)]
        up_to, onward = [masked[0]], [masked[-1]]
        for c in range(1, channels):
            up_to.append(up_to[-1] + masked[c])
            onward.append(onward[-1] + masked[channels - 1 - c])
        for c in range(channels):
            up, down = onward[channels - 1 - c], up_to[c]
            across_ref[c, part] = jnp.where(odd_block, up, down).astype(across_ref.dtype)
            inside_ref[c, part] = jnp.where(odd_block, down, up).astype(inside_ref.dtype)
            own_ref[c, part] = up_to[-1] + (1.0 - flags[c]) * plain[c]


def covariances(first, flags, voltages, size):
    channels, _, ports, samples = voltages.shape
    folded = (channels, size + size // 2, LANES)
    smem = pl.BlockSpec(memory_space=pltpu.SMEM)
    vmem = pl.BlockSpec(memory_space=pltpu.VMEM)
    return pl.pallas_call(
        covariance_kernel,
        in_specs=[smem, smem, pl.BlockSpec(memory_space=pltpu.HBM)],
        out_specs=[vmem] * 3,
        scratch_shapes=[
            pltpu.VMEM((channels, ports, 2, samples), voltages.dtype),
            pltpu.VMEM((channels, 2, 2 * size, LANES), jnp.float32),
            pltpu.VMEM((channels, 2, size, LANES), jnp.float32),
            pltpu.VMEM(folded, jnp.float32),
            pltpu.SemaphoreType.DMA((channels,)),
        ],
        out_shape=[
            jax.ShapeDtypeStruct(folded, jnp.bfloat16),
            jax.ShapeDtypeStruct(folded, jnp.bfloat16),
            jax.ShapeDtypeStruct(folded, jnp.float32),
        ],
        compiler_params=pltpu.CompilerParams(vmem_limit_bytes=56 * 1024 * 1024),
    )(first, flags, jnp.transpose(voltages, (0, 2, 1, 3)))


def window_kernel(slab_ref, own_ref, inside_ref, across_ref, mine_ref, *sent_refs):
    share = mine_ref.shape[0]

    def window(slab):
        rows = pl.ds(slab * share, share)
        ends = inside_ref[rows].astype(jnp.float32) + across_ref[rows].astype(jnp.float32)
        return own_ref[rows] + ends

    mine_ref[...] = window(slab_ref[0])
    for turn, sent_ref in enumerate(sent_refs, 1):
        sent_ref[...] = window(slab_ref[0] ^ turn).astype(sent_ref.dtype)


def windows(slab, own, inside, across, slabs):
    shape = (own.shape[0] // slabs,) + own.shape[1:]
    return pl.pallas_call(
        window_kernel,
        in_specs=[pl.BlockSpec(memory_space=pltpu.SMEM)]
        + [pl.BlockSpec(own.shape, lambda: (0, 0, 0))] * 3,
        out_specs=[pl.BlockSpec(shape, lambda: (0, 0, 0))] * slabs,
        out_shape=[jax.ShapeDtypeStruct(shape, jnp.float32)]
        + [jax.ShapeDtypeStruct(shape, jnp.bfloat16)] * (slabs - 1),
        compiler_params=pltpu.CompilerParams(vmem_limit_bytes=VMEM_LIMIT),
    )(slab, own, inside, across)


def choose_kernel(slab_ref, index_ref, steer_ref, out_ref):
    beams, half = index_ref.shape[0], out_ref.shape[1] // 2
    ports = steer_ref.shape[3]
    out_ref[...] = jnp.zeros_like(out_ref)
    for channel in range(out_ref.shape[0]):
        for part in range(2):
            for beam in range(beams):
                row = steer_ref[channel, part, pl.ds(index_ref[beam], 1), :]
                out_ref[channel, pl.ds(part * half + beam, 1), pl.ds(0, ports)] = row


def chosen_vectors(slab, beam_index, steering, share, half, size):
    directions, ports = steering.shape[2:]
    return pl.pallas_call(
        choose_kernel,
        grid_spec=pltpu.PrefetchScalarGridSpec(
            num_scalar_prefetch=2,
            grid=(1,),
            in_specs=[
                pl.BlockSpec((share, 2, directions, ports), lambda i, slab, _: (slab[0], 0, 0, 0))
            ],
            out_specs=pl.BlockSpec((share, 2 * half, size), lambda i, *_: (0, 0, 0)),
        ),
        out_shape=jax.ShapeDtypeStruct((share, 2 * half, size), jnp.float32),
        compiler_params=pltpu.CompilerParams(vmem_limit_bytes=VMEM_LIMIT),
    )(slab, beam_index, steering)


def unpack(folded):
    packed = unfold(folded)
    size = packed.shape[0]
    half = size // 2
    row, col = iotas(size, 2 * LANES)
    spread = (row == jnp.where(col < LANES, 2 * col, 2 * (col - LANES) + 1)) & (col % LANES < half)
    spread = spread.astype(jnp.float32).astype(jnp.bfloat16)
    high, rest = split(packed)
    lowest = packed - high.astype(jnp.float32) - rest.astype(jnp.float32)
    parts = dot_nn(jnp.concatenate([high, rest, lowest.astype(jnp.bfloat16)], axis=0), spread)
    parts = parts[:size] + (parts[size : 2 * size] + parts[2 * size :])
    real, imag = parts[:, :half], parts[:, LANES : LANES + half]
    row, col = iotas(half, half)
    turned_real, turned_imag = real[:half].T, imag[:half].T
    first_real = jnp.where(row >= col, real[:half], turned_real)
    first_imag = jnp.where(row > col, imag[:half], jnp.where(row < col, -turned_imag, 0.0))
    second_real = jnp.where(row < col, real[:half], jnp.where(row > col, turned_real, imag[:half]))
    second_imag = jnp.where(row < col, imag[:half], jnp.where(row > col, -turned_imag, 0.0))

    def blocks(first, second, low, high):
        return jnp.concatenate(
            [jnp.concatenate([first, high], axis=1), jnp.concatenate([low, second], axis=1)], axis=0
        )

    low_real, low_imag = real[half:], imag[half:]
    return (
        blocks(first_real, second_real, low_real, low_real.T),
        blocks(first_imag, second_imag, low_imag, -low_imag.T),
    )


def gains(bound, steps):
    spread, out = (bound - 1.0) / (bound + 1.0), []
    for _ in range(steps):
        centre = spread * spread / 2
        out.append((spread, 1.0 / (1.0 - centre)))
        spread = centre / (1.0 - centre)
    return out


def stack(*arrays):
    return jnp.concatenate(arrays, axis=0)


def apply(y, real, imag, passes):
    n = y.shape[0]
    half = n // 2
    if passes == 1:
        with_real = dot_nn(y.astype(jnp.bfloat16), real.astype(jnp.bfloat16))
        with_imag = dot_nn(y.astype(jnp.bfloat16), imag.astype(jnp.bfloat16))
    else:
        (rh, rl), (ih, il), (yh, yl) = split(real), split(imag), split(y)
        by_rh, by_ih = dot_nn(stack(yh, yl), rh), dot_nn(stack(yh, yl), ih)
        with_real = by_rh[:n] + by_rh[n:] + dot_nn(yh, rl)
        with_imag = by_ih[:n] + by_ih[n:] + dot_nn(yh, il)
    return stack(with_real[:half] + with_imag[half:], with_real[half:] - with_imag[:half])


def square(real, imag, passes):
    n = real.shape[0]
    if passes == 1:
        rh, ih = real.astype(jnp.bfloat16), imag.astype(jnp.bfloat16)
        by_ih = dot_nn(stack(ih, rh), ih)
        rr, ii, ri = dot_nn(rh, rh), by_ih[:n], by_ih[n:]
    else:
        (rh, rl), (ih, il) = split(real), split(imag)
        by_rh, by_rl = dot_nn(stack(rh, rl), rh), dot_nn(rh, rl)
        by_ih, by_il = dot_nn(stack(ih, il, rh, rl), ih), dot_nn(stack(ih, rh), il)
        rr = by_rh[:n] + by_rh[n:] + by_rl
        ii = by_ih[:n] + by_ih[n : 2 * n] + by_il[:n]
        ri = by_ih[2 * n : 3 * n] + by_ih[3 * n :] + by_il[n:]
    return rr - ii, ri - ri.T


def solve_kernel(ports, beams, first_ref, flags_ref, *refs):
    own_ref, *got_refs, chosen_ref, weight_ref = refs
    share, half, size = weight_ref.shape[0], chosen_ref.shape[1] // 2, chosen_ref.shape[2]
    bound = ports / LOADING + 1.0
    row, col = iotas(size, size)
    identity = jnp.where(row == col, 1.0, 0.0)
    channels = range(share)
    state = []
    for c in channels:
        folded = own_ref[c]
        for got_ref in got_refs:
            folded = folded + got_ref[c].astype(jnp.float32)
        real, imag = unpack(folded)
        trace = jnp.sum(jnp.sum(real * identity, axis=0, keepdims=True), axis=1, keepdims=True)
        loading = trace * (LOADING / ports)
        scale = 2.0 / (loading * (1.0 + bound))
        real = real + jnp.where((row == col) & (row < ports), loading, 0.0)
        state.append((real * scale, imag * scale, chosen_ref[c] * scale))
    steps = gains(bound, SQUARINGS)
    for number, (spread, gain) in enumerate(steps):
        squares = number + 1 < len(steps)
        for c in channels:
            real, imag, y = state[c]
            if number == len(steps) - 2:
                real, imag = identity - real, -imag
            if number < len(steps) - 2:
                new_y = gain * (2.0 * y - apply(y, real, imag, 3))
                real2, imag2 = square(real, imag, 3)
                real, imag = gain * (2.0 * real - real2), gain * (2.0 * imag - imag2)
            else:
                new_y = gain * (y + apply(y, real, imag, 3 if squares else 1))
                if squares:
                    real, imag = square(real, imag, 1)
                    real = gain * (real - identity * (spread * spread / 2))
                    imag = gain * imag
            state[c] = real, imag, new_y
    beam = lax.broadcasted_iota(jnp.int32, (half, 1), 0)
    row, col = iotas(2 * half, 2 * half)
    place = jnp.where(row % 2 == 0, row // 2, row // 2 + half)
    order = jnp.where(col == place, jnp.where(row % 2 == 0, 1.0, -1.0), 0.0).astype(jnp.bfloat16)
    for c in channels:
        y = state[c][2]
        sums = jnp.sum(y * chosen_ref[c], axis=1, keepdims=True)
        denominator = jnp.where(beam < beams, sums[:half] + sums[half:], 1.0)
        flag = flags_ref[first_ref[0] + c].astype(jnp.float32)
        factor = jnp.where(beam < beams, flag / denominator, 0.0)
        weights = dot_nn(order, (y * stack(factor, factor)).astype(jnp.bfloat16))
        high = weights[:, LANES:]
        weight_ref[c, : 2 * half] = weights[:, :LANES].astype(jnp.bfloat16)
        weight_ref[c, 2 * half :] = jnp.concatenate([high[:half], high[half:]], axis=1).astype(
            jnp.bfloat16
        )


def solved_weights(first, flags, own, got, chosen, ports, beams):
    share, rows, _ = chosen.shape
    smem = pl.BlockSpec(memory_space=pltpu.SMEM)
    whole = [pl.BlockSpec(a.shape, lambda: (0, 0, 0)) for a in (own, *got, chosen)]
    shape = (share, rows + rows // 2, LANES)
    return pl.pallas_call(
        functools.partial(solve_kernel, ports, beams),
        in_specs=[smem, smem] + whole,
        out_specs=pl.BlockSpec(shape, lambda: (0, 0, 0)),
        out_shape=jax.ShapeDtypeStruct(shape, jnp.bfloat16),
        compiler_params=pltpu.CompilerParams(vmem_limit_bytes=VMEM_LIMIT),
    )(first, flags, own, *got, chosen)


def beam_kernel(slab_ref, volt_ref, *refs):
    *weight_refs, out_ref, mixed = refs
    share, rows, _ = weight_refs[0].shape
    rows = rows * 2 // 3
    _, ports, _, samples = volt_ref.shape
    together, beams = out_ref.shape[:2]
    step = pl.program_id(0)

    @pl.when(step == 0)
    def _():
        folded = [ref[c].astype(jnp.float32) for ref in weight_refs for c in range(share)]
        real_rows = stack(*[unfold(f) for f in folded])
        count, size = real_rows.shape
        row, _ = iotas(count, size)
        below, above = pltpu.roll(real_rows, count - 1, 0), pltpu.roll(real_rows, 1, 0)
        imag_rows = jnp.where(row % 2 == 0, -below, above)
        row, col = iotas(size, 2 * ports)
        to_even = (col == 2 * row).astype(jnp.float32).astype(jnp.bfloat16)
        to_odd = (col == 2 * row + 1).astype(jnp.float32).astype(jnp.bfloat16)
        placed = dot_nn(real_rows.astype(jnp.bfloat16), to_even)
        placed = (placed + dot_nn(imag_rows.astype(jnp.bfloat16), to_odd)).astype(jnp.bfloat16)
        for turn in range(len(weight_refs)):
            first = (slab_ref[0] ^ turn) * share
            for c in range(share):
                at = (turn * share + c) * rows
                mixed[first + c] = placed[at : at + rows]

    for c in range(together):
        channel = step * together + c
        formed = dot_nn(mixed[channel], volt_ref[channel].reshape(2 * ports, samples))
        out_ref[c] = formed[: 2 * beams].astype(jnp.bfloat16).reshape(beams, 2, samples)


def formed_beams(slab, voltages, weights, beams):
    channels, _, ports, samples = voltages.shape
    rows = weights[0].shape[1] * 2 // 3
    together = 2
    whole = pl.BlockSpec(weights[0].shape, lambda i: (0, 0, 0))
    out = pl.pallas_call(
        beam_kernel,
        grid=(channels // together,),
        in_specs=[pl.BlockSpec(memory_space=pltpu.SMEM), pl.BlockSpec(memory_space=pltpu.VMEM)]
        + [whole] * len(weights),
        out_specs=pl.BlockSpec((together, beams, 2, samples), lambda i: (i, 0, 0, 0)),
        scratch_shapes=[pltpu.VMEM((channels, rows, 2 * ports), jnp.bfloat16)],
        out_shape=jax.ShapeDtypeStruct((channels, beams, 2, samples), jnp.bfloat16),
        compiler_params=pltpu.CompilerParams(vmem_limit_bytes=VMEM_LIMIT),
    )(slab, jnp.transpose(voltages, (0, 2, 1, 3)), *weights)
    return jnp.transpose(out, (0, 2, 1, 3))


def body(voltages, steering, beam_index, channel_flags):
    channel_count, _, port_count, _ = voltages.shape
    beam_count = beam_index.shape[0]
    slabs, blocks = lax.axis_size("slab"), lax.axis_size("chan")
    if channel_count != HW or slabs & (slabs - 1) or not LANES < port_count <= LANES * 3 // 2:
        raise ValueError("unsupported mesh")
    share = channel_count // slabs
    size = LANES + LANES // 2
    half = round_up(beam_count, 8)
    slab = lax.axis_index("slab").astype(jnp.int32).reshape(1)
    first_channel = (lax.axis_index("chan") * channel_count).astype(jnp.int32).reshape(1)
    chosen = chosen_vectors(slab, beam_index, steering, share, half, size)
    across, inside, own = covariances(first_channel, channel_flags, voltages, size)
    pairs = [[(i, i + 1) for i in range(start, blocks - 1, 2)] for start in range(2)]
    inside_pairs, across_pairs = [ahead + [(j, i) for i, j in ahead] for ahead in pairs]
    across = lax.ppermute(across, "chan", across_pairs)
    inside = lax.ppermute(inside, "chan", inside_pairs)
    mine, *sent = windows(slab, own, inside, across, slabs)

    def swap(arrays):
        return [
            lax.ppermute(array, "slab", [(i, i ^ turn) for i in range(slabs)])
            for turn, array in enumerate(arrays, 1)
        ]

    got = swap(sent)
    first_share = first_channel + slab * share
    weights = solved_weights(first_share, channel_flags, mine, got, chosen, port_count, beam_count)
    others = swap([weights] * (slabs - 1))
    return formed_beams(slab, voltages, [weights, *others], beam_count)


def solution(mesh):
    return jax.shard_map(
        body,
        mesh=mesh,
        in_specs=(P("chan", None, None, "slab"), P("chan", None, None, None), P(), P()),
        out_specs=P("chan", None, None, "slab"),
        check_vma=False,
    )
```

```python
import functools

import jax
import jax.numpy as jnp
from jax import lax
from jax.experimental import pallas as pl
from jax.experimental.pallas import tpu as pltpu
from jax.sharding import PartitionSpec as P

HW = 8


LOADING = 0.1

LANES = 128
VMEM_LIMIT = 24 * 1024 * 1024
SQUARINGS = 8


def round_up(value, multiple):
    return -(-value // multiple) * multiple


def dot_nn(left, right):
    return lax.dot_general(
        left, right, (((1,), (0,)), ((), ())), preferred_element_type=jnp.float32
    )


def dot_nt(left, right):
    return lax.dot_general(
        left, right, (((1,), (1,)), ((), ())), preferred_element_type=jnp.float32
    )


def iotas(rows, cols):
    return (
        lax.broadcasted_iota(jnp.int32, (rows, cols), 0),
        lax.broadcasted_iota(jnp.int32, (rows, cols), 1),
    )


def unfold(folded):
    size = folded.shape[0] * 2 // 3
    width = LANES // 2
    rest = jnp.concatenate([folded[size:, :width], folded[size:, width:]], axis=0)
    return jnp.concatenate([folded[:size], rest], axis=1)


def split(x):
    high = x.astype(jnp.bfloat16)
    return high, (x - high.astype(jnp.float32)).astype(jnp.bfloat16)


def combine(even_rows, odd_rows):
    lane = lax.broadcasted_iota(jnp.int32, even_rows.shape, 1)
    real = even_rows + pltpu.roll(odd_rows, LANES - 1, 1)
    return jnp.where(lane % 2 == 0, real, pltpu.roll(odd_rows, 1, 1) - even_rows)


def gram(volt, left_ref, right_ref):
    lead = left_ref.shape[1] // 2
    rest = volt.shape[0] - lead
    left, right = dot_nt(volt, volt[:lead]), dot_nt(volt[lead:], volt[lead:])
    left_ref[0, : volt.shape[0]] = left[:, :LANES]
    left_ref[1, : volt.shape[0], : lead - LANES] = left[:, LANES:]
    right_ref[0, :rest] = right[:, :LANES]
    right_ref[1, :rest, : rest - LANES] = right[:, LANES:]


def pack(left_ref, right_ref, out_ref):
    half = left_ref.shape[1] // 4

    def rows(ref, lanes, first, parity):
        return ref[lanes, pl.ds(2 * first + parity, half, stride=2), :]

    top = []
    for lanes in range(2):
        row, lane = iotas(half, LANES)
        gap = lane + lanes * LANES - 2 * row
        first = [rows(left_ref, lanes, 0, parity) for parity in range(2)]
        second = [rows(right_ref, lanes, 0, parity) for parity in range(2)]
        even = jnp.where(gap <= 0, first[0], jnp.where(gap == 1, -second[1], second[0]))
        odd = jnp.where(gap == 0, second[0], jnp.where(gap <= 1, first[1], second[1]))
        top.append((even, odd))
    low = [[rows(left_ref, lanes, half, parity) for parity in range(2)] for lanes in range(2)]
    width = LANES // 2
    side = [
        jnp.concatenate([above[:, :width], below[:, :width]], axis=1)
        for above, below in zip(top[1], low[1])
    ]
    for place, pair in enumerate((top[0], low[0], side)):
        out_ref[place * half : (place + 1) * half] = combine(*pair)


def covariance_kernel(
    first_ref,
    flags_hbm,
    volt_hbm,
    across_ref,
    inside_ref,
    own_ref,
    volts,
    lefts,
    rights,
    kept,
    flags_ref,
    sems,
    flags_sem,
):
    channels, ports, _, samples = volts.shape
    copies = [
        pltpu.make_async_copy(volt_hbm.at[c], volts.at[c], sems.at[c]) for c in range(channels)
    ]
    flags_copy = pltpu.make_async_copy(flags_hbm, flags_ref, flags_sem)
    flags_copy.start()
    groups = [range(c, c + 2) for c in range(0, channels, 2)]
    for group in groups[:2]:
        for c in group:
            copies[c].start()
    lefts[...] = jnp.zeros_like(lefts)
    rights[...] = jnp.zeros_like(rights)
    for number, group in enumerate(groups):
        for c in group:
            copies[c].wait()
        for later in groups[number + 2 : number + 3]:
            for c in later:
                copies[c].start()
        for c in group:
            gram(volts[c].reshape(2 * ports, samples), lefts.at[c % 4], rights.at[c % 4])
        for c in groups[number - 1] if number else ():
            pack(lefts.at[c % 4], rights.at[c % 4], kept.at[c])
    for c in groups[-1]:
        pack(lefts.at[c % 4], rights.at[c % 4], kept.at[c])
    flags_copy.wait()
    flags = [flags_ref[first_ref[0] + c].astype(jnp.float32) for c in range(channels)]
    odd_block = (first_ref[0] // channels) % 2 == 1
    for start in range(0, kept.shape[1], 16):
        part = slice(start, start + 16)
        plain = [kept[c, part] for c in range(channels)]
        masked = [plain[c] * flags[c] for c in range(channels)]
        up_to, onward = [masked[0]], [masked[-1]]
        for c in range(1, channels):
            up_to.append(up_to[-1] + masked[c])
            onward.append(onward[-1] + masked[channels - 1 - c])
        for c in range(channels):
            up, down = onward[channels - 1 - c], up_to[c]
            across_ref[c, part] = jnp.where(odd_block, up, down).astype(across_ref.dtype)
            inside_ref[c, part] = jnp.where(odd_block, down, up).astype(inside_ref.dtype)
            own_ref[c, part] = up_to[-1] + (1.0 - flags[c]) * plain[c]


def covariances(first, flags, voltages, size):
    channels, ports, _, samples = voltages.shape
    folded = (channels, size + size // 2, LANES)
    smem = pl.BlockSpec(memory_space=pltpu.SMEM)
    vmem = pl.BlockSpec(memory_space=pltpu.VMEM)
    return pl.pallas_call(
        covariance_kernel,
        in_specs=[smem] + [pl.BlockSpec(memory_space=pltpu.HBM)] * 2,
        out_specs=[vmem] * 4,
        scratch_shapes=[
            pltpu.VMEM((4, 2, 2 * size, LANES), jnp.float32),
            pltpu.VMEM((4, 2, size, LANES), jnp.float32),
            pltpu.VMEM(folded, jnp.float32),
            pltpu.SMEM(flags.shape, flags.dtype),
            pltpu.SemaphoreType.DMA((channels,)),
            pltpu.SemaphoreType.DMA,
        ],
        out_shape=[
            pltpu.VMEM(folded, jnp.bfloat16),
            pltpu.VMEM(folded, jnp.bfloat16),
            pltpu.VMEM(folded, jnp.float32),
            pltpu.VMEM(voltages.shape, voltages.dtype),
        ],
        compiler_params=pltpu.CompilerParams(vmem_limit_bytes=VMEM_LIMIT),
    )(first, *[pltpu.with_memory_space_constraint(a, pltpu.HBM) for a in (flags, voltages)])


def window_kernel(slab_ref, own_ref, inside_ref, across_ref, mine_ref, *sent_refs):
    share = mine_ref.shape[0]

    def window(slab):
        rows = pl.ds(slab * share, share)
        ends = inside_ref[rows].astype(jnp.float32) + across_ref[rows].astype(jnp.float32)
        return own_ref[rows] + ends

    mine_ref[...] = window(slab_ref[0])
    for turn, sent_ref in enumerate(sent_refs, 1):
        sent_ref[...] = window(slab_ref[0] ^ turn).astype(sent_ref.dtype)


def windows(slab, own, inside, across, slabs):
    shape = (own.shape[0] // slabs,) + own.shape[1:]
    return pl.pallas_call(
        window_kernel,
        in_specs=[pl.BlockSpec(memory_space=pltpu.SMEM)]
        + [pl.BlockSpec(own.shape, lambda: (0, 0, 0))] * 3,
        out_specs=[pl.BlockSpec(shape, lambda: (0, 0, 0))] * slabs,
        out_shape=[jax.ShapeDtypeStruct(shape, jnp.float32)]
        + [jax.ShapeDtypeStruct(shape, jnp.bfloat16)] * (slabs - 1),
        compiler_params=pltpu.CompilerParams(vmem_limit_bytes=VMEM_LIMIT),
    )(slab, own, inside, across)


def choose_kernel(slab_ref, index_ref, steer_ref, out_ref):
    beams, half = index_ref.shape[0], out_ref.shape[1] // 2
    ports = steer_ref.shape[3]
    out_ref[...] = jnp.zeros_like(out_ref)
    for channel in range(out_ref.shape[0]):
        for part in range(2):
            for beam in range(beams):
                row = steer_ref[channel, part, pl.ds(index_ref[beam], 1), :]
                out_ref[channel, pl.ds(part * half + beam, 1), pl.ds(0, ports)] = row


def chosen_vectors(slab, beam_index, steering, share, half, size):
    directions, ports = steering.shape[2:]
    return pl.pallas_call(
        choose_kernel,
        grid_spec=pltpu.PrefetchScalarGridSpec(
            num_scalar_prefetch=2,
            grid=(1,),
            in_specs=[
                pl.BlockSpec((share, 2, directions, ports), lambda i, slab, _: (slab[0], 0, 0, 0))
            ],
            out_specs=pl.BlockSpec((share, 2 * half, size), lambda i, *_: (0, 0, 0)),
        ),
        out_shape=jax.ShapeDtypeStruct((share, 2 * half, size), jnp.float32),
        compiler_params=pltpu.CompilerParams(vmem_limit_bytes=VMEM_LIMIT),
    )(slab, beam_index, steering)


def unpack(folded):
    packed = unfold(folded)
    size = packed.shape[0]
    half = size // 2
    row, col = iotas(size, 2 * LANES)
    spread = (row == jnp.where(col < LANES, 2 * col, 2 * (col - LANES) + 1)) & (col % LANES < half)
    spread = spread.astype(jnp.float32).astype(jnp.bfloat16)
    high, rest = split(packed)
    lowest = packed - high.astype(jnp.float32) - rest.astype(jnp.float32)
    parts = dot_nn(jnp.concatenate([high, rest, lowest.astype(jnp.bfloat16)], axis=0), spread)
    parts = parts[:size] + (parts[size : 2 * size] + parts[2 * size :])
    real, imag = parts[:, :half], parts[:, LANES : LANES + half]
    row, col = iotas(half, half)
    turned_real, turned_imag = real[:half].T, imag[:half].T
    first_real = jnp.where(row >= col, real[:half], turned_real)
    first_imag = jnp.where(row > col, imag[:half], jnp.where(row < col, -turned_imag, 0.0))
    second_real = jnp.where(row < col, real[:half], jnp.where(row > col, turned_real, imag[:half]))
    second_imag = jnp.where(row < col, imag[:half], jnp.where(row > col, -turned_imag, 0.0))

    def blocks(first, second, low, high):
        return jnp.concatenate(
            [jnp.concatenate([first, high], axis=1), jnp.concatenate([low, second], axis=1)], axis=0
        )

    low_real, low_imag = real[half:], imag[half:]
    return (
        blocks(first_real, second_real, low_real, low_real.T),
        blocks(first_imag, second_imag, low_imag, -low_imag.T),
    )


def gains(bound, steps):
    spread, out = (bound - 1.0) / (bound + 1.0), []
    for _ in range(steps):
        centre = spread * spread / 2
        out.append((spread, 1.0 / (1.0 - centre)))
        spread = centre / (1.0 - centre)
    return out


def stack(*arrays):
    return jnp.concatenate(arrays, axis=0)


def multiply(y, real, imag, squares=True):
    n, m = y.shape[0], real.shape[0]
    half = n // 2
    (rh, rl), (ih, il), (yh, yl) = split(real), split(imag), split(y)
    if squares:
        by_rh, by_rl = dot_nn(stack(yh, yl, rh, rl), rh), dot_nn(stack(yh, rh), rl)
        by_ih, by_il = dot_nn(stack(yh, yl, ih, il), ih), dot_nn(stack(yh, ih, rh), il)
        cross = dot_nn(stack(rh, rl), ih)
    else:
        by_rh, by_rl = dot_nn(stack(yh, yl), rh), dot_nn(yh, rl)
        by_ih, by_il = dot_nn(stack(yh, yl), ih), dot_nn(yh, il)
    with_real = by_rh[:n] + by_rh[n : 2 * n] + by_rl[:n]
    with_imag = by_ih[:n] + by_ih[n : 2 * n] + by_il[:n]
    product = stack(with_real[:half] + with_imag[half:], with_real[half:] - with_imag[:half])
    if not squares:
        return product, None, None
    by_rh, by_rl, by_ih, by_il = by_rh[2 * n :], by_rl[n:], by_ih[2 * n :], by_il[n:]
    rr = by_rh[:m] + by_rh[m:] + by_rl
    ii = by_ih[:m] + by_ih[m:] + by_il[:m]
    ri = cross[:m] + cross[m:] + by_il[m:]
    return product, rr - ii, ri - ri.T


def multiply_once(y, real, imag, squares):
    n, m = y.shape[0], real.shape[0]
    half = n // 2
    rh, ih, yh = (a.astype(jnp.bfloat16) for a in (real, imag, y))
    by_rh = dot_nn(stack(yh, rh) if squares else yh, rh)
    by_ih = dot_nn(stack(yh, ih, rh) if squares else yh, ih)
    product = stack(by_rh[:half] + by_ih[half:n], by_rh[half:n] - by_ih[:half])
    if not squares:
        return product, None, None
    ri = by_ih[n + m :]
    return product, by_rh[n:] - by_ih[n : n + m], ri - ri.T


def solve_kernel(ports, beams, first_ref, flags_ref, *refs):
    own_ref, *got_refs, chosen_ref, weight_ref = refs
    share, half, size = weight_ref.shape[0], chosen_ref.shape[1] // 2, chosen_ref.shape[2]
    bound = ports / LOADING + 1.0
    row, col = iotas(size, size)
    identity = jnp.where(row == col, 1.0, 0.0)
    channels = range(share)
    state = []
    for c in channels:
        folded = own_ref[c]
        for got_ref in got_refs:
            folded = folded + got_ref[c].astype(jnp.float32)
        real, imag = unpack(folded)
        trace = jnp.sum(jnp.sum(real * identity, axis=0, keepdims=True), axis=1, keepdims=True)
        loading = trace * (LOADING / ports)
        scale = 2.0 / (loading * (1.0 + bound))
        real = real + jnp.where((row == col) & (row < ports), loading, 0.0)
        state.append((real * scale, imag * scale, chosen_ref[c] * scale))
    steps = gains(bound, SQUARINGS)
    for number, (spread, gain) in enumerate(steps):
        squares = number + 1 < len(steps)
        for c in channels:
            real, imag, y = state[c]
            if number == len(steps) - 2:
                real, imag = identity - real, -imag
            if number < len(steps) - 2:
                product, real2, imag2 = multiply(y, real, imag)
                y = gain * (2.0 * y - product)
                real, imag = gain * (2.0 * real - real2), gain * (2.0 * imag - imag2)
            elif squares:
                product, _, _ = multiply(y, real, imag, squares=False)
                _, real, imag = multiply_once(y, real, imag, True)
                y = gain * (y + product)
                real, imag = gain * (real - identity * (spread * spread / 2)), gain * imag
            else:
                y = gain * (y + multiply_once(y, real, imag, False)[0])
            state[c] = real, imag, y
    beam = lax.broadcasted_iota(jnp.int32, (half, 1), 0)
    row, col = iotas(2 * half, 2 * half)
    place = jnp.where(row % 2 == 0, row // 2, row // 2 + half)
    order = jnp.where(col == place, jnp.where(row % 2 == 0, 1.0, -1.0), 0.0).astype(jnp.bfloat16)
    for c in channels:
        y = state[c][2]
        sums = jnp.sum(y * chosen_ref[c], axis=1, keepdims=True)
        denominator = jnp.where(beam < beams, sums[:half] + sums[half:], 1.0)
        flag = flags_ref[first_ref[0] + c].astype(jnp.float32)
        factor = jnp.where(beam < beams, flag / denominator, 0.0)
        weights = dot_nn(order, (y * stack(factor, factor)).astype(jnp.bfloat16))
        high = weights[:, LANES:]
        weight_ref[c, : 2 * half] = weights[:, :LANES].astype(jnp.bfloat16)
        weight_ref[c, 2 * half :] = jnp.concatenate([high[:half], high[half:]], axis=1).astype(
            jnp.bfloat16
        )


def solved_weights(first, flags, own, got, chosen, ports, beams):
    share, rows, _ = chosen.shape
    smem = pl.BlockSpec(memory_space=pltpu.SMEM)
    whole = [pl.BlockSpec(a.shape, lambda: (0, 0, 0)) for a in (own, *got, chosen)]
    shape = (share, rows + rows // 2, LANES)
    return pl.pallas_call(
        functools.partial(solve_kernel, ports, beams),
        in_specs=[smem, smem] + whole,
        out_specs=pl.BlockSpec(shape, lambda: (0, 0, 0)),
        out_shape=jax.ShapeDtypeStruct(shape, jnp.bfloat16),
        compiler_params=pltpu.CompilerParams(vmem_limit_bytes=VMEM_LIMIT),
    )(first, flags, own, *got, chosen)


def beam_kernel(slab_ref, volt_ref, *refs):
    *weight_refs, out_ref, mixed = refs
    share, rows, _ = weight_refs[0].shape
    rows = rows * 2 // 3
    _, ports, _, samples = volt_ref.shape
    together, beams = out_ref.shape[:2]
    step = pl.program_id(0)

    @pl.when(step == 0)
    def _():
        folded = [ref[c].astype(jnp.float32) for ref in weight_refs for c in range(share)]
        real_rows = stack(*[unfold(f) for f in folded])
        count, size = real_rows.shape
        row, _ = iotas(count, size)
        below, above = pltpu.roll(real_rows, count - 1, 0), pltpu.roll(real_rows, 1, 0)
        imag_rows = jnp.where(row % 2 == 0, -below, above)
        row, col = iotas(size, 2 * ports)
        to_even = (col == 2 * row).astype(jnp.float32).astype(jnp.bfloat16)
        to_odd = (col == 2 * row + 1).astype(jnp.float32).astype(jnp.bfloat16)
        placed = dot_nn(real_rows.astype(jnp.bfloat16), to_even)
        placed = (placed + dot_nn(imag_rows.astype(jnp.bfloat16), to_odd)).astype(jnp.bfloat16)
        for turn in range(len(weight_refs)):
            first = (slab_ref[0] ^ turn) * share
            for c in range(share):
                at = (turn * share + c) * rows
                mixed[first + c] = placed[at : at + rows]

    for c in range(together):
        channel = step * together + c
        formed = dot_nn(mixed[channel], volt_ref[channel].reshape(2 * ports, samples))
        out_ref[c] = formed[: 2 * beams].astype(jnp.bfloat16).reshape(beams, 2, samples)


def formed_beams(slab, voltages, weights, beams):
    channels, ports, _, samples = voltages.shape
    rows = weights[0].shape[1] * 2 // 3
    together = 4
    whole = pl.BlockSpec(weights[0].shape, lambda i: (0, 0, 0))
    return pl.pallas_call(
        beam_kernel,
        grid=(channels // together,),
        in_specs=[pl.BlockSpec(memory_space=pltpu.SMEM), pl.BlockSpec(memory_space=pltpu.VMEM)]
        + [whole] * len(weights),
        out_specs=pl.BlockSpec((together, beams, 2, samples), lambda i: (i, 0, 0, 0)),
        scratch_shapes=[pltpu.VMEM((channels, rows, 2 * ports), jnp.bfloat16)],
        out_shape=jax.ShapeDtypeStruct((channels, beams, 2, samples), jnp.bfloat16),
        compiler_params=pltpu.CompilerParams(vmem_limit_bytes=VMEM_LIMIT),
    )(slab, voltages, *weights)


def body(voltages, steering, beam_index, channel_flags):
    channel_count, _, port_count, _ = voltages.shape
    beam_count = beam_index.shape[0]
    slabs, blocks = lax.axis_size("slab"), lax.axis_size("chan")
    if channel_count != HW or slabs & (slabs - 1) or not LANES < port_count <= LANES * 3 // 2:
        raise ValueError("unsupported mesh")
    share = channel_count // slabs
    size = LANES + LANES // 2
    half = round_up(beam_count, 8)
    slab = lax.axis_index("slab").astype(jnp.int32).reshape(1)
    first_channel = (lax.axis_index("chan") * channel_count).astype(jnp.int32).reshape(1)
    chosen = chosen_vectors(slab, beam_index, steering, share, half, size)
    by_port = jnp.transpose(voltages, (0, 2, 1, 3))
    across, inside, own, held = covariances(first_channel, channel_flags, by_port, size)
    pairs = [[(i, i + 1) for i in range(start, blocks - 1, 2)] for start in range(2)]
    inside_pairs, across_pairs = [ahead + [(j, i) for i, j in ahead] for ahead in pairs]
    across = lax.ppermute(across, "chan", across_pairs)
    inside = lax.ppermute(inside, "chan", inside_pairs)
    mine, *sent = windows(slab, own, inside, across, slabs)

    def swap(arrays):
        return [
            lax.ppermute(array, "slab", [(i, i ^ turn) for i in range(slabs)])
            for turn, array in enumerate(arrays, 1)
        ]

    got = swap(sent)
    first_share = first_channel + slab * share
    weights = solved_weights(first_share, channel_flags, mine, got, chosen, port_count, beam_count)
    others = swap([weights] * (slabs - 1))
    beams = formed_beams(slab, held, [weights, *others], beam_count)
    return jnp.transpose(beams, (0, 2, 1, 3))


def solution(mesh):
    return jax.shard_map(
        body,
        mesh=mesh,
        in_specs=(P("chan", None, None, "slab"), P("chan", None, None, None), P(), P()),
        out_specs=P("chan", None, None, "slab"),
        check_vma=False,
    )
```

```python
import functools

import jax
import jax.numpy as jnp
from jax import lax
from jax.experimental import pallas as pl
from jax.experimental.pallas import tpu as pltpu
from jax.sharding import PartitionSpec as P

HW = 8


LOADING = 0.1

LANES = 128
VMEM_LIMIT = 24 * 1024 * 1024
SQUARINGS = 8


def round_up(value, multiple):
    return -(-value // multiple) * multiple


def dot_nn(left, right):
    return lax.dot_general(
        left, right, (((1,), (0,)), ((), ())), preferred_element_type=jnp.float32
    )


def dot_nt(left, right):
    return lax.dot_general(
        left, right, (((1,), (1,)), ((), ())), preferred_element_type=jnp.float32
    )


def iotas(rows, cols):
    return (
        lax.broadcasted_iota(jnp.int32, (rows, cols), 0),
        lax.broadcasted_iota(jnp.int32, (rows, cols), 1),
    )


def unfold(folded):
    size = folded.shape[0] * 2 // 3
    width = LANES // 2
    rest = jnp.concatenate([folded[size:, :width], folded[size:, width:]], axis=0)
    return jnp.concatenate([folded[:size], rest], axis=1)


def split(x):
    high = x.astype(jnp.bfloat16)
    return high, (x - high.astype(jnp.float32)).astype(jnp.bfloat16)


def combine(even_rows, odd_rows):
    lane = lax.broadcasted_iota(jnp.int32, even_rows.shape, 1)
    real = even_rows + pltpu.roll(odd_rows, LANES - 1, 1)
    return jnp.where(lane % 2 == 0, real, pltpu.roll(odd_rows, 1, 1) - even_rows)


def gram(volt, left_ref, right_ref):
    lead = left_ref.shape[1] // 2
    rest = volt.shape[0] - lead
    left, right = dot_nt(volt, volt[:lead]), dot_nt(volt[lead:], volt[lead:])
    left_ref[0, : volt.shape[0]] = left[:, :LANES]
    left_ref[1, : volt.shape[0], : lead - LANES] = left[:, LANES:]
    right_ref[0, :rest] = right[:, :LANES]
    right_ref[1, :rest, : rest - LANES] = right[:, LANES:]


def pack(left_ref, right_ref, out_ref):
    half = left_ref.shape[1] // 4

    def rows(ref, lanes, first, parity):
        return ref[lanes, pl.ds(2 * first + parity, half, stride=2), :]

    top = []
    for lanes in range(2):
        row, lane = iotas(half, LANES)
        gap = lane + lanes * LANES - 2 * row
        first = [rows(left_ref, lanes, 0, parity) for parity in range(2)]
        second = [rows(right_ref, lanes, 0, parity) for parity in range(2)]
        even = jnp.where(gap <= 0, first[0], jnp.where(gap == 1, -second[1], second[0]))
        odd = jnp.where(gap == 0, second[0], jnp.where(gap <= 1, first[1], second[1]))
        top.append((even, odd))
    low = [[rows(left_ref, lanes, half, parity) for parity in range(2)] for lanes in range(2)]
    width = LANES // 2
    side = [
        jnp.concatenate([above[:, :width], below[:, :width]], axis=1)
        for above, below in zip(top[1], low[1])
    ]
    for place, pair in enumerate((top[0], low[0], side)):
        out_ref[place * half : (place + 1) * half] = combine(*pair)


def covariance_kernel(
    first_ref,
    flags_hbm,
    volt_hbm,
    across_ref,
    inside_ref,
    own_ref,
    volts,
    lefts,
    rights,
    kept,
    flags_ref,
    sems,
    flags_sem,
):
    channels, ports, _, samples = volts.shape
    copies = [
        pltpu.make_async_copy(volt_hbm.at[c], volts.at[c], sems.at[c]) for c in range(channels)
    ]
    flags_copy = pltpu.make_async_copy(flags_hbm, flags_ref, flags_sem)
    flags_copy.start()
    groups = [range(c, c + 2) for c in range(0, channels, 2)]
    for group in groups[:2]:
        for c in group:
            copies[c].start()
    lefts[...] = jnp.zeros_like(lefts)
    rights[...] = jnp.zeros_like(rights)
    for number, group in enumerate(groups):
        for c in group:
            copies[c].wait()
        for later in groups[number + 2 : number + 3]:
            for c in later:
                copies[c].start()
        for c in group:
            gram(volts[c].reshape(2 * ports, samples), lefts.at[c % 4], rights.at[c % 4])
        for c in groups[number - 1] if number else ():
            pack(lefts.at[c % 4], rights.at[c % 4], kept.at[c])
    for c in groups[-1]:
        pack(lefts.at[c % 4], rights.at[c % 4], kept.at[c])
    flags_copy.wait()
    flags = [flags_ref[first_ref[0] + c].astype(jnp.float32) for c in range(channels)]
    odd_block = (first_ref[0] // channels) % 2 == 1
    for start in range(0, kept.shape[1], 16):
        part = slice(start, start + 16)
        plain = [kept[c, part] for c in range(channels)]
        masked = [plain[c] * flags[c] for c in range(channels)]
        up_to, onward = [masked[0]], [masked[-1]]
        for c in range(1, channels):
            up_to.append(up_to[-1] + masked[c])
            onward.append(onward[-1] + masked[channels - 1 - c])
        for c in range(channels):
            up, down = onward[channels - 1 - c], up_to[c]
            across_ref[c, part] = jnp.where(odd_block, up, down).astype(across_ref.dtype)
            inside_ref[c, part] = jnp.where(odd_block, down, up).astype(inside_ref.dtype)
            own_ref[c, part] = up_to[-1] + (1.0 - flags[c]) * plain[c]


def covariances(first, flags, voltages, size):
    channels, ports, _, samples = voltages.shape
    folded = (channels, size + size // 2, LANES)
    smem = pl.BlockSpec(memory_space=pltpu.SMEM)
    vmem = pl.BlockSpec(memory_space=pltpu.VMEM)
    return pl.pallas_call(
        covariance_kernel,
        in_specs=[smem] + [pl.BlockSpec(memory_space=pltpu.HBM)] * 2,
        out_specs=[vmem] * 3,
        scratch_shapes=[
            pltpu.VMEM(voltages.shape, voltages.dtype),
            pltpu.VMEM((4, 2, 2 * size, LANES), jnp.float32),
            pltpu.VMEM((4, 2, size, LANES), jnp.float32),
            pltpu.VMEM(folded, jnp.float32),
            pltpu.SMEM(flags.shape, flags.dtype),
            pltpu.SemaphoreType.DMA((channels,)),
            pltpu.SemaphoreType.DMA,
        ],
        out_shape=[
            pltpu.VMEM(folded, jnp.bfloat16),
            pltpu.VMEM(folded, jnp.bfloat16),
            pltpu.VMEM(folded, jnp.float32),
        ],
        compiler_params=pltpu.CompilerParams(vmem_limit_bytes=VMEM_LIMIT),
    )(first, *[pltpu.with_memory_space_constraint(a, pltpu.HBM) for a in (flags, voltages)])


def window_kernel(slab_ref, own_ref, inside_ref, across_ref, mine_ref, *sent_refs):
    share = mine_ref.shape[0]

    def window(slab):
        rows = pl.ds(slab * share, share)
        ends = inside_ref[rows].astype(jnp.float32) + across_ref[rows].astype(jnp.float32)
        return own_ref[rows] + ends

    mine_ref[...] = window(slab_ref[0])
    for turn, sent_ref in enumerate(sent_refs, 1):
        sent_ref[...] = window(slab_ref[0] ^ turn).astype(sent_ref.dtype)


def windows(slab, own, inside, across, slabs):
    shape = (own.shape[0] // slabs,) + own.shape[1:]
    return pl.pallas_call(
        window_kernel,
        in_specs=[pl.BlockSpec(memory_space=pltpu.SMEM)]
        + [pl.BlockSpec(own.shape, lambda: (0, 0, 0))] * 3,
        out_specs=[pl.BlockSpec(shape, lambda: (0, 0, 0))] * slabs,
        out_shape=[jax.ShapeDtypeStruct(shape, jnp.float32)]
        + [jax.ShapeDtypeStruct(shape, jnp.bfloat16)] * (slabs - 1),
        compiler_params=pltpu.CompilerParams(vmem_limit_bytes=VMEM_LIMIT),
    )(slab, own, inside, across)


def choose_kernel(slab_ref, index_ref, steer_ref, out_ref):
    beams, half = index_ref.shape[0], out_ref.shape[1] // 2
    ports = steer_ref.shape[3]
    out_ref[...] = jnp.zeros_like(out_ref)
    for channel in range(out_ref.shape[0]):
        for part in range(2):
            for beam in range(beams):
                row = steer_ref[channel, part, pl.ds(index_ref[beam], 1), :]
                out_ref[channel, pl.ds(part * half + beam, 1), pl.ds(0, ports)] = row


def chosen_vectors(slab, beam_index, steering, share, half, size):
    directions, ports = steering.shape[2:]
    return pl.pallas_call(
        choose_kernel,
        grid_spec=pltpu.PrefetchScalarGridSpec(
            num_scalar_prefetch=2,
            grid=(1,),
            in_specs=[
                pl.BlockSpec((share, 2, directions, ports), lambda i, slab, _: (slab[0], 0, 0, 0))
            ],
            out_specs=pl.BlockSpec((share, 2 * half, size), lambda i, *_: (0, 0, 0)),
        ),
        out_shape=jax.ShapeDtypeStruct((share, 2 * half, size), jnp.float32),
        compiler_params=pltpu.CompilerParams(vmem_limit_bytes=VMEM_LIMIT),
    )(slab, beam_index, steering)


def unpack(folded):
    packed = unfold(folded)
    size = packed.shape[0]
    half = size // 2
    row, col = iotas(size, 2 * LANES)
    spread = (row == jnp.where(col < LANES, 2 * col, 2 * (col - LANES) + 1)) & (col % LANES < half)
    spread = spread.astype(jnp.float32).astype(jnp.bfloat16)
    high, rest = split(packed)
    lowest = packed - high.astype(jnp.float32) - rest.astype(jnp.float32)
    parts = dot_nn(jnp.concatenate([high, rest, lowest.astype(jnp.bfloat16)], axis=0), spread)
    parts = parts[:size] + (parts[size : 2 * size] + parts[2 * size :])
    real, imag = parts[:, :half], parts[:, LANES : LANES + half]
    row, col = iotas(half, half)
    turned_real, turned_imag = real[:half].T, imag[:half].T
    first_real = jnp.where(row >= col, real[:half], turned_real)
    first_imag = jnp.where(row > col, imag[:half], jnp.where(row < col, -turned_imag, 0.0))
    second_real = jnp.where(row < col, real[:half], jnp.where(row > col, turned_real, imag[:half]))
    second_imag = jnp.where(row < col, imag[:half], jnp.where(row > col, -turned_imag, 0.0))

    def blocks(first, second, low, high):
        return jnp.concatenate(
            [jnp.concatenate([first, high], axis=1), jnp.concatenate([low, second], axis=1)], axis=0
        )

    low_real, low_imag = real[half:], imag[half:]
    return (
        blocks(first_real, second_real, low_real, low_real.T),
        blocks(first_imag, second_imag, low_imag, -low_imag.T),
    )


def gains(bound, steps):
    spread, out = (bound - 1.0) / (bound + 1.0), []
    for _ in range(steps):
        centre = spread * spread / 2
        out.append((spread, 1.0 / (1.0 - centre)))
        spread = centre / (1.0 - centre)
    return out


def stack(*arrays):
    return jnp.concatenate(arrays, axis=0)


def multiply(y, real, imag, squares=True):
    n, m = y.shape[0], real.shape[0]
    half = n // 2
    (rh, rl), (ih, il), (yh, yl) = split(real), split(imag), split(y)
    if squares:
        by_rh, by_rl = dot_nn(stack(yh, yl, rh, rl), rh), dot_nn(stack(yh, rh), rl)
        by_ih, by_il = dot_nn(stack(yh, yl, ih, il), ih), dot_nn(stack(yh, ih, rh), il)
        cross = dot_nn(stack(rh, rl), ih)
    else:
        by_rh, by_rl = dot_nn(stack(yh, yl), rh), dot_nn(yh, rl)
        by_ih, by_il = dot_nn(stack(yh, yl), ih), dot_nn(yh, il)
    with_real = by_rh[:n] + by_rh[n : 2 * n] + by_rl[:n]
    with_imag = by_ih[:n] + by_ih[n : 2 * n] + by_il[:n]
    product = stack(with_real[:half] + with_imag[half:], with_real[half:] - with_imag[:half])
    if not squares:
        return product, None, None
    by_rh, by_rl, by_ih, by_il = by_rh[2 * n :], by_rl[n:], by_ih[2 * n :], by_il[n:]
    rr = by_rh[:m] + by_rh[m:] + by_rl
    ii = by_ih[:m] + by_ih[m:] + by_il[:m]
    ri = cross[:m] + cross[m:] + by_il[m:]
    return product, rr - ii, ri - ri.T


def multiply_once(y, real, imag, squares):
    n, m = y.shape[0], real.shape[0]
    half = n // 2
    rh, ih, yh = (a.astype(jnp.bfloat16) for a in (real, imag, y))
    by_rh = dot_nn(stack(yh, rh) if squares else yh, rh)
    by_ih = dot_nn(stack(yh, ih, rh) if squares else yh, ih)
    product = stack(by_rh[:half] + by_ih[half:n], by_rh[half:n] - by_ih[:half])
    if not squares:
        return product, None, None
    ri = by_ih[n + m :]
    return product, by_rh[n:] - by_ih[n : n + m], ri - ri.T


def solve_kernel(ports, beams, first_ref, flags_ref, held_ref, *refs):
    own_ref, *got_refs, chosen_ref, weight_ref = refs
    share, half, size = weight_ref.shape[0], chosen_ref.shape[1] // 2, chosen_ref.shape[2]
    bound = ports / LOADING + 1.0
    row, col = iotas(size, size)
    identity = jnp.where(row == col, 1.0, 0.0)
    channels = range(share)
    state = []
    for c in channels:
        folded = own_ref[c]
        for got_ref in got_refs:
            folded = folded + got_ref[c].astype(jnp.float32)
        real, imag = unpack(folded)
        trace = jnp.sum(jnp.sum(real * identity, axis=0, keepdims=True), axis=1, keepdims=True)
        loading = trace * (LOADING / ports)
        scale = 2.0 / (loading * (1.0 + bound))
        real = real + jnp.where((row == col) & (row < ports), loading, 0.0)
        state.append((real * scale, imag * scale, chosen_ref[c] * scale))
    steps = gains(bound, SQUARINGS)
    for number, (spread, gain) in enumerate(steps):
        squares = number + 1 < len(steps)
        for c in channels:
            real, imag, y = state[c]
            if number == len(steps) - 2:
                real, imag = identity - real, -imag
            if number < len(steps) - 2:
                product, real2, imag2 = multiply(y, real, imag)
                y = gain * (2.0 * y - product)
                real, imag = gain * (2.0 * real - real2), gain * (2.0 * imag - imag2)
            elif squares:
                product, _, _ = multiply(y, real, imag, squares=False)
                _, real, imag = multiply_once(y, real, imag, True)
                y = gain * (y + product)
                real, imag = gain * (real - identity * (spread * spread / 2)), gain * imag
            else:
                y = gain * (y + multiply_once(y, real, imag, False)[0])
            state[c] = real, imag, y
    beam = lax.broadcasted_iota(jnp.int32, (half, 1), 0)
    row, col = iotas(2 * half, 2 * half)
    place = jnp.where(row % 2 == 0, row // 2, row // 2 + half)
    order = jnp.where(col == place, jnp.where(row % 2 == 0, 1.0, -1.0), 0.0).astype(jnp.bfloat16)
    for c in channels:
        y = state[c][2]
        sums = jnp.sum(y * chosen_ref[c], axis=1, keepdims=True)
        denominator = jnp.where(beam < beams, sums[:half] + sums[half:], 1.0)
        flag = flags_ref[first_ref[0] + c].astype(jnp.float32)
        factor = jnp.where(beam < beams, flag / denominator, 0.0)
        weights = dot_nn(order, (y * stack(factor, factor)).astype(jnp.bfloat16))
        high = weights[:, LANES:]
        weight_ref[c, : 2 * half] = weights[:, :LANES].astype(jnp.bfloat16)
        weight_ref[c, 2 * half :] = jnp.concatenate([high[:half], high[half:]], axis=1).astype(
            jnp.bfloat16
        )


def solved_weights(first, flags, held, own, got, chosen, ports, beams):
    share, rows, _ = chosen.shape
    smem = pl.BlockSpec(memory_space=pltpu.SMEM)
    whole = [pl.BlockSpec(a.shape, lambda: (0, 0, 0)) for a in (own, *got, chosen)]
    shape = (share, rows + rows // 2, LANES)
    return pl.pallas_call(
        functools.partial(solve_kernel, ports, beams),
        in_specs=[smem, smem, pl.BlockSpec(memory_space=pl.ANY)] + whole,
        out_specs=pl.BlockSpec(shape, lambda: (0, 0, 0)),
        out_shape=jax.ShapeDtypeStruct(shape, jnp.bfloat16),
        compiler_params=pltpu.CompilerParams(vmem_limit_bytes=VMEM_LIMIT),
    )(first, flags, held, own, *got, chosen)


def hold_kernel(volt_hbm, weight_hbm, held_ref, sems):
    copies = [
        pltpu.make_async_copy(volt_hbm.at[c], held_ref.at[c], sems.at[c])
        for c in range(held_ref.shape[0])
    ]
    for copy in copies:
        copy.start()
    for copy in copies:
        copy.wait()


def held_voltages(voltages, weights):
    return pl.pallas_call(
        hold_kernel,
        in_specs=[pl.BlockSpec(memory_space=pltpu.HBM), pl.BlockSpec(memory_space=pl.ANY)],
        out_specs=pl.BlockSpec(memory_space=pltpu.VMEM),
        scratch_shapes=[pltpu.SemaphoreType.DMA((voltages.shape[0],))],
        out_shape=pltpu.VMEM(voltages.shape, voltages.dtype),
        compiler_params=pltpu.CompilerParams(vmem_limit_bytes=VMEM_LIMIT),
    )(pltpu.with_memory_space_constraint(voltages, pltpu.HBM), weights)


def beam_kernel(first_turn, slab_ref, volt_ref, *refs):
    *weight_refs, out_ref, mixed = refs if first_turn == 0 else refs[1:]
    share, rows, _ = weight_refs[0].shape
    rows = rows * 2 // 3
    _, ports, _, samples = volt_ref.shape
    beams = out_ref.shape[1]
    step = pl.program_id(0)

    @pl.when(step == 0)
    def _():
        folded = [ref[c].astype(jnp.float32) for ref in weight_refs for c in range(share)]
        real_rows = stack(*[unfold(f) for f in folded])
        count, size = real_rows.shape
        row, _ = iotas(count, size)
        below, above = pltpu.roll(real_rows, count - 1, 0), pltpu.roll(real_rows, 1, 0)
        imag_rows = jnp.where(row % 2 == 0, -below, above)
        row, col = iotas(size, 2 * ports)
        to_even = (col == 2 * row).astype(jnp.float32).astype(jnp.bfloat16)
        to_odd = (col == 2 * row + 1).astype(jnp.float32).astype(jnp.bfloat16)
        placed = dot_nn(real_rows.astype(jnp.bfloat16), to_even)
        placed = (placed + dot_nn(imag_rows.astype(jnp.bfloat16), to_odd)).astype(jnp.bfloat16)
        for number in range(len(folded)):
            mixed[number] = placed[number * rows : (number + 1) * rows]

    first = (slab_ref[0] ^ (step + first_turn)) * share
    for c in range(share):
        volt = volt_ref[first + c].reshape(2 * ports, samples)
        formed = dot_nn(mixed[step * share + c], volt)
        out_ref[c] = formed[: 2 * beams].astype(jnp.bfloat16).reshape(beams, 2, samples)


def formed_beams(slab, voltages, weights, beams, formed=None):
    channels, ports, _, samples = voltages.shape
    share, rows, _ = weights[0].shape
    first_turn = 0 if formed is None else 1
    before = [] if formed is None else [formed]
    whole = pl.BlockSpec(weights[0].shape, lambda i, _: (0, 0, 0))
    return pl.pallas_call(
        functools.partial(beam_kernel, first_turn),
        grid_spec=pltpu.PrefetchScalarGridSpec(
            num_scalar_prefetch=1,
            grid=(len(weights),),
            in_specs=[pl.BlockSpec(memory_space=pltpu.VMEM)]
            + [pl.BlockSpec(memory_space=pl.ANY)] * len(before)
            + [whole] * len(weights),
            out_specs=pl.BlockSpec(
                (share, beams, 2, samples), lambda i, slab: (slab[0] ^ (i + first_turn), 0, 0, 0)
            ),
            scratch_shapes=[
                pltpu.VMEM((len(weights) * share, rows * 2 // 3, 2 * ports), jnp.bfloat16)
            ],
        ),
        out_shape=jax.ShapeDtypeStruct((channels, beams, 2, samples), jnp.bfloat16),
        input_output_aliases={} if formed is None else {2: 0},
        compiler_params=pltpu.CompilerParams(vmem_limit_bytes=VMEM_LIMIT),
    )(slab, voltages, *before, *weights)


def body(voltages, steering, beam_index, channel_flags):
    channel_count, _, port_count, _ = voltages.shape
    beam_count = beam_index.shape[0]
    slabs, blocks = lax.axis_size("slab"), lax.axis_size("chan")
    if channel_count != HW or slabs & (slabs - 1) or not LANES < port_count <= LANES * 3 // 2:
        raise ValueError("unsupported mesh")
    share = channel_count // slabs
    size = LANES + LANES // 2
    half = round_up(beam_count, 8)
    slab = lax.axis_index("slab").astype(jnp.int32).reshape(1)
    first_channel = (lax.axis_index("chan") * channel_count).astype(jnp.int32).reshape(1)
    chosen = chosen_vectors(slab, beam_index, steering, share, half, size)
    by_port = jnp.transpose(voltages, (0, 2, 1, 3))
    across, inside, own = covariances(first_channel, channel_flags, by_port, size)
    pairs = [[(i, i + 1) for i in range(start, blocks - 1, 2)] for start in range(2)]
    inside_pairs, across_pairs = [ahead + [(j, i) for i, j in ahead] for ahead in pairs]
    across = lax.ppermute(across, "chan", across_pairs)
    inside = lax.ppermute(inside, "chan", inside_pairs)
    mine, *sent = windows(slab, own, inside, across, slabs)

    def swap(arrays):
        return [
            lax.ppermute(array, "slab", [(i, i ^ turn) for i in range(slabs)])
            for turn, array in enumerate(arrays, 1)
        ]

    got = swap(sent)
    held = held_voltages(by_port, mine)
    first_share = first_channel + slab * share
    weights = solved_weights(first_share, channel_flags, held, mine, got, chosen, port_count, beam_count)
    others = swap([weights] * (slabs - 1))
    beams = formed_beams(slab, held, [weights], beam_count)
    beams = formed_beams(slab, held, others, beam_count, beams)
    return jnp.transpose(beams, (0, 2, 1, 3))


def solution(mesh):
    return jax.shard_map(
        body,
        mesh=mesh,
        in_specs=(P("chan", None, None, "slab"), P("chan", None, None, None), P(), P()),
        out_specs=P("chan", None, None, "slab"),
        check_vma=False,
    )
```

```python
import functools

import jax
import jax.numpy as jnp
from jax import lax
from jax.experimental import pallas as pl
from jax.experimental.pallas import tpu as pltpu
from jax.sharding import PartitionSpec as P

HW = 8


LOADING = 0.1

LANES = 128
VMEM_LIMIT = 24 * 1024 * 1024
SQUARINGS = 8


def round_up(value, multiple):
    return -(-value // multiple) * multiple


def dot_nn(left, right):
    return lax.dot_general(
        left, right, (((1,), (0,)), ((), ())), preferred_element_type=jnp.float32
    )


def dot_nt(left, right):
    return lax.dot_general(
        left, right, (((1,), (1,)), ((), ())), preferred_element_type=jnp.float32
    )


def iotas(rows, cols):
    return (
        lax.broadcasted_iota(jnp.int32, (rows, cols), 0),
        lax.broadcasted_iota(jnp.int32, (rows, cols), 1),
    )


def unfold(folded):
    size = folded.shape[0] * 2 // 3
    width = LANES // 2
    rest = jnp.concatenate([folded[size:, :width], folded[size:, width:]], axis=0)
    return jnp.concatenate([folded[:size], rest], axis=1)


def split(x):
    high = x.astype(jnp.bfloat16)
    return high, (x - high.astype(jnp.float32)).astype(jnp.bfloat16)


def combine(even_rows, odd_rows):
    lane = lax.broadcasted_iota(jnp.int32, even_rows.shape, 1)
    real = even_rows + pltpu.roll(odd_rows, LANES - 1, 1)
    return jnp.where(lane % 2 == 0, real, pltpu.roll(odd_rows, 1, 1) - even_rows)


def gram(volt, left_ref, right_ref):
    lead = left_ref.shape[1] // 2
    rest = volt.shape[0] - lead
    left, right = dot_nt(volt, volt[:lead]), dot_nt(volt[lead:], volt[lead:])
    left_ref[0, : volt.shape[0]] = left[:, :LANES]
    left_ref[1, : volt.shape[0], : lead - LANES] = left[:, LANES:]
    right_ref[0, :rest] = right[:, :LANES]
    right_ref[1, :rest, : rest - LANES] = right[:, LANES:]


def pack(left_ref, right_ref, out_ref):
    half = left_ref.shape[1] // 4

    def rows(ref, lanes, first, parity):
        return ref[lanes, pl.ds(2 * first + parity, half, stride=2), :]

    top = []
    for lanes in range(2):
        row, lane = iotas(half, LANES)
        gap = lane + lanes * LANES - 2 * row
        first = [rows(left_ref, lanes, 0, parity) for parity in range(2)]
        second = [rows(right_ref, lanes, 0, parity) for parity in range(2)]
        even = jnp.where(gap <= 0, first[0], jnp.where(gap == 1, -second[1], second[0]))
        odd = jnp.where(gap == 0, second[0], jnp.where(gap <= 1, first[1], second[1]))
        top.append((even, odd))
    low = [[rows(left_ref, lanes, half, parity) for parity in range(2)] for lanes in range(2)]
    width = LANES // 2
    side = [
        jnp.concatenate([above[:, :width], below[:, :width]], axis=1)
        for above, below in zip(top[1], low[1])
    ]
    for place, pair in enumerate((top[0], low[0], side)):
        out_ref[place * half : (place + 1) * half] = combine(*pair)


def covariance_kernel(
    first_ref,
    flags_hbm,
    volt_hbm,
    across_ref,
    inside_lead_ref,
    inside_rest_ref,
    own_ref,
    volts,
    lefts,
    rights,
    kept,
    flags_ref,
    sems,
    flags_sem,
):
    channels, ports, _, samples = volts.shape
    half = inside_lead_ref.shape[0]
    copies = [
        pltpu.make_async_copy(volt_hbm.at[c], volts.at[c], sems.at[c]) for c in range(channels)
    ]
    flags_copy = pltpu.make_async_copy(flags_hbm, flags_ref, flags_sem)
    flags_copy.start()
    groups = [range(c, c + 2) for c in range(0, channels, 2)]
    for group in groups[:2]:
        for c in group:
            copies[c].start()
    lefts[...] = jnp.zeros_like(lefts)
    rights[...] = jnp.zeros_like(rights)
    for number, group in enumerate(groups):
        for c in group:
            copies[c].wait()
        for later in groups[number + 2 : number + 3]:
            for c in later:
                copies[c].start()
        for c in group:
            gram(volts[c].reshape(2 * ports, samples), lefts.at[c % 4], rights.at[c % 4])
        for c in groups[number - 1] if number else ():
            pack(lefts.at[c % 4], rights.at[c % 4], kept.at[c])
    for c in groups[-1]:
        pack(lefts.at[c % 4], rights.at[c % 4], kept.at[c])
    flags_copy.wait()
    flags = [flags_ref[first_ref[0] + c].astype(jnp.float32) for c in range(channels)]
    odd_block = (first_ref[0] // channels) % 2 == 1
    for start in range(0, kept.shape[1], 16):
        part = slice(start, start + 16)
        plain = [kept[c, part] for c in range(channels)]
        masked = [plain[c] * flags[c] for c in range(channels)]
        up_to, onward = [masked[0]], [masked[-1]]
        for c in range(1, channels):
            up_to.append(up_to[-1] + masked[c])
            onward.append(onward[-1] + masked[channels - 1 - c])
        for c in range(channels):
            up, down = onward[channels - 1 - c], up_to[c]
            across_ref[c, part] = jnp.where(odd_block, up, down).astype(across_ref.dtype)
            inside = jnp.where(odd_block, down, up).astype(across_ref.dtype)
            if c < half:
                inside_lead_ref[c, part] = inside
            else:
                inside_rest_ref[c - half, part] = inside
            own_ref[c, part] = up_to[-1] + (1.0 - flags[c]) * plain[c]


def covariances(first, flags, voltages, size):
    channels, ports, _, samples = voltages.shape
    folded = (channels, size + size // 2, LANES)
    half = channels // 2
    smem = pl.BlockSpec(memory_space=pltpu.SMEM)
    vmem = pl.BlockSpec(memory_space=pltpu.VMEM)
    return pl.pallas_call(
        covariance_kernel,
        in_specs=[smem] + [pl.BlockSpec(memory_space=pltpu.HBM)] * 2,
        out_specs=[vmem] * 4,
        scratch_shapes=[
            pltpu.VMEM(voltages.shape, voltages.dtype),
            pltpu.VMEM((4, 2, 2 * size, LANES), jnp.float32),
            pltpu.VMEM((4, 2, size, LANES), jnp.float32),
            pltpu.VMEM(folded, jnp.float32),
            pltpu.SMEM(flags.shape, flags.dtype),
            pltpu.SemaphoreType.DMA((channels,)),
            pltpu.SemaphoreType.DMA,
        ],
        out_shape=[
            pltpu.VMEM(folded, jnp.bfloat16),
            pltpu.VMEM((half, *folded[1:]), jnp.bfloat16),
            pltpu.VMEM((channels - half, *folded[1:]), jnp.bfloat16),
            pltpu.VMEM(folded, jnp.float32),
        ],
        compiler_params=pltpu.CompilerParams(vmem_limit_bytes=VMEM_LIMIT),
    )(first, *[pltpu.with_memory_space_constraint(a, pltpu.HBM) for a in (flags, voltages)])


def window_kernel(slab_ref, own_ref, across_ref, inside_lead_ref, inside_rest_ref, *refs):
    mine_ref, *sent_refs, sums = refs
    share = mine_ref.shape[0]
    half = inside_lead_ref.shape[0]
    for c in range(own_ref.shape[0]):
        inside = inside_lead_ref[c] if c < half else inside_rest_ref[c - half]
        ends = inside.astype(jnp.float32) + across_ref[c].astype(jnp.float32)
        sums[c] = own_ref[c] + ends

    def window(slab):
        return sums[pl.ds(slab * share, share)]

    mine_ref[...] = window(slab_ref[0])
    for turn, sent_ref in enumerate(sent_refs, 1):
        sent_ref[...] = window(slab_ref[0] ^ turn).astype(sent_ref.dtype)


def windows(slab, own, across, inside_lead, inside_rest, slabs):
    arrays = own, across, inside_lead, inside_rest
    shape = (own.shape[0] // slabs,) + own.shape[1:]
    return pl.pallas_call(
        window_kernel,
        in_specs=[pl.BlockSpec(memory_space=pltpu.SMEM)]
        + [pl.BlockSpec(a.shape, lambda: (0, 0, 0)) for a in arrays],
        out_specs=[pl.BlockSpec(shape, lambda: (0, 0, 0))] * slabs,
        out_shape=[jax.ShapeDtypeStruct(shape, jnp.float32)]
        + [jax.ShapeDtypeStruct(shape, jnp.bfloat16)] * (slabs - 1),
        scratch_shapes=[pltpu.VMEM(own.shape, jnp.float32)],
        compiler_params=pltpu.CompilerParams(vmem_limit_bytes=VMEM_LIMIT),
    )(slab, *arrays)


def choose_kernel(slab_ref, index_ref, steer_ref, out_ref):
    beams, half = index_ref.shape[0], out_ref.shape[1] // 2
    ports = steer_ref.shape[3]
    out_ref[...] = jnp.zeros_like(out_ref)
    for channel in range(out_ref.shape[0]):
        for part in range(2):
            for beam in range(beams):
                row = steer_ref[channel, part, pl.ds(index_ref[beam], 1), :]
                out_ref[channel, pl.ds(part * half + beam, 1), pl.ds(0, ports)] = row


def chosen_vectors(slab, beam_index, steering, share, half, size):
    directions, ports = steering.shape[2:]
    return pl.pallas_call(
        choose_kernel,
        grid_spec=pltpu.PrefetchScalarGridSpec(
            num_scalar_prefetch=2,
            grid=(1,),
            in_specs=[
                pl.BlockSpec((share, 2, directions, ports), lambda i, slab, _: (slab[0], 0, 0, 0))
            ],
            out_specs=pl.BlockSpec((share, 2 * half, size), lambda i, *_: (0, 0, 0)),
        ),
        out_shape=jax.ShapeDtypeStruct((share, 2 * half, size), jnp.float32),
        compiler_params=pltpu.CompilerParams(vmem_limit_bytes=VMEM_LIMIT),
    )(slab, beam_index, steering)


def unpack(folded):
    packed = unfold(folded)
    size = packed.shape[0]
    half = size // 2
    row, col = iotas(size, 2 * LANES)
    spread = (row == jnp.where(col < LANES, 2 * col, 2 * (col - LANES) + 1)) & (col % LANES < half)
    spread = spread.astype(jnp.float32).astype(jnp.bfloat16)
    high, rest = split(packed)
    lowest = packed - high.astype(jnp.float32) - rest.astype(jnp.float32)
    parts = dot_nn(jnp.concatenate([high, rest, lowest.astype(jnp.bfloat16)], axis=0), spread)
    parts = parts[:size] + (parts[size : 2 * size] + parts[2 * size :])
    real, imag = parts[:, :half], parts[:, LANES : LANES + half]
    row, col = iotas(half, half)
    turned_real, turned_imag = real[:half].T, imag[:half].T
    first_real = jnp.where(row >= col, real[:half], turned_real)
    first_imag = jnp.where(row > col, imag[:half], jnp.where(row < col, -turned_imag, 0.0))
    second_real = jnp.where(row < col, real[:half], jnp.where(row > col, turned_real, imag[:half]))
    second_imag = jnp.where(row < col, imag[:half], jnp.where(row > col, -turned_imag, 0.0))

    def blocks(first, second, low, high):
        return jnp.concatenate(
            [jnp.concatenate([first, high], axis=1), jnp.concatenate([low, second], axis=1)], axis=0
        )

    low_real, low_imag = real[half:], imag[half:]
    return (
        blocks(first_real, second_real, low_real, low_real.T),
        blocks(first_imag, second_imag, low_imag, -low_imag.T),
    )


def gains(bound, steps):
    spread, out = (bound - 1.0) / (bound + 1.0), []
    for _ in range(steps):
        centre = spread * spread / 2
        out.append((spread, 1.0 / (1.0 - centre)))
        spread = centre / (1.0 - centre)
    return out


def stack(*arrays):
    return jnp.concatenate(arrays, axis=0)


def multiply(y, real, imag, squares=True):
    n, m = y.shape[0], real.shape[0]
    half = n // 2
    (rh, rl), (ih, il), (yh, yl) = split(real), split(imag), split(y)
    if squares:
        by_rh, by_rl = dot_nn(stack(yh, yl, rh), rh), dot_nn(stack(yh, rh), rl)
        by_ih, by_il = dot_nn(stack(yh, yl, ih), ih), dot_nn(yh, il)
    else:
        by_rh, by_rl = dot_nn(stack(yh, yl), rh), dot_nn(yh, rl)
        by_ih, by_il = dot_nn(stack(yh, yl), ih), dot_nn(yh, il)
    with_real = by_rh[:n] + by_rh[n : 2 * n] + by_rl[:n]
    with_imag = by_ih[:n] + by_ih[n : 2 * n] + by_il
    product = stack(with_real[:half] + with_imag[half:], with_real[half:] - with_imag[:half])
    if not squares:
        return product, None, None
    cross = dot_nn(stack(rh, rl), ih)
    mixed = by_rl[n:] - dot_nn(ih, il)
    rr_less_ii = by_rh[2 * n :] - by_ih[2 * n :] + (mixed + mixed.T)
    ri = cross[:m] + cross[m:] + dot_nn(rh, il)
    return product, rr_less_ii, ri - ri.T


def multiply_once(y, real, imag, squares):
    n, m = y.shape[0], real.shape[0]
    half = n // 2
    rh, ih, yh = (a.astype(jnp.bfloat16) for a in (real, imag, y))
    by_rh = dot_nn(stack(yh, rh) if squares else yh, rh)
    by_ih = dot_nn(stack(yh, ih, rh) if squares else yh, ih)
    product = stack(by_rh[:half] + by_ih[half:n], by_rh[half:n] - by_ih[:half])
    if not squares:
        return product, None, None
    ri = by_ih[n + m :]
    return product, by_rh[n:] - by_ih[n : n + m], ri - ri.T


def solve_kernel(ports, beams, first_ref, flags_ref, held_ref, *refs):
    own_ref, *got_refs, chosen_ref, weight_ref = refs
    share, half, size = weight_ref.shape[0], chosen_ref.shape[1] // 2, chosen_ref.shape[2]
    bound = ports / LOADING + 1.0
    row, col = iotas(size, size)
    identity = jnp.where(row == col, 1.0, 0.0)
    channels = range(share)
    state = []
    for c in channels:
        folded = own_ref[c]
        for got_ref in got_refs:
            folded = folded + got_ref[c].astype(jnp.float32)
        real, imag = unpack(folded)
        trace = jnp.sum(jnp.sum(real * identity, axis=0, keepdims=True), axis=1, keepdims=True)
        loading = trace * (LOADING / ports)
        scale = 2.0 / (loading * (1.0 + bound))
        real = real + jnp.where((row == col) & (row < ports), loading, 0.0)
        state.append((real * scale, imag * scale, chosen_ref[c] * scale))
    steps = gains(bound, SQUARINGS)
    for number, (spread, gain) in enumerate(steps):
        squares = number + 1 < len(steps)
        for c in channels:
            real, imag, y = state[c]
            if number == len(steps) - 2:
                real, imag = identity - real, -imag
            if number < len(steps) - 2:
                product, real2, imag2 = multiply(y, real, imag)
                y = gain * (2.0 * y - product)
                real, imag = gain * (2.0 * real - real2), gain * (2.0 * imag - imag2)
            elif squares:
                product, _, _ = multiply(y, real, imag, squares=False)
                _, real, imag = multiply_once(y, real, imag, True)
                y = gain * (y + product)
                real, imag = gain * (real - identity * (spread * spread / 2)), gain * imag
            else:
                y = gain * (y + multiply_once(y, real, imag, False)[0])
            state[c] = real, imag, y
    beam = lax.broadcasted_iota(jnp.int32, (half, 1), 0)
    row, col = iotas(2 * half, 2 * half)
    place = jnp.where(row % 2 == 0, row // 2, row // 2 + half)
    order = jnp.where(col == place, jnp.where(row % 2 == 0, 1.0, -1.0), 0.0).astype(jnp.bfloat16)
    for c in channels:
        y = state[c][2]
        sums = jnp.sum(y * chosen_ref[c], axis=1, keepdims=True)
        denominator = jnp.where(beam < beams, sums[:half] + sums[half:], 1.0)
        flag = flags_ref[first_ref[0] + c].astype(jnp.float32)
        factor = jnp.where(beam < beams, flag / denominator, 0.0)
        weights = dot_nn(order, (y * stack(factor, factor)).astype(jnp.bfloat16))
        high = weights[:, LANES:]
        weight_ref[c, : 2 * half] = weights[:, :LANES].astype(jnp.bfloat16)
        weight_ref[c, 2 * half :] = jnp.concatenate([high[:half], high[half:]], axis=1).astype(
            jnp.bfloat16
        )


def solved_weights(first, flags, held, own, got, chosen, ports, beams):
    share, rows, _ = chosen.shape
    smem = pl.BlockSpec(memory_space=pltpu.SMEM)
    whole = [pl.BlockSpec(a.shape, lambda: (0, 0, 0)) for a in (own, *got, chosen)]
    shape = (share, rows + rows // 2, LANES)
    return pl.pallas_call(
        functools.partial(solve_kernel, ports, beams),
        in_specs=[smem, smem, pl.BlockSpec(memory_space=pl.ANY)] + whole,
        out_specs=pl.BlockSpec(shape, lambda: (0, 0, 0)),
        out_shape=jax.ShapeDtypeStruct(shape, jnp.bfloat16),
        compiler_params=pltpu.CompilerParams(vmem_limit_bytes=VMEM_LIMIT),
    )(first, flags, held, own, *got, chosen)


def hold_kernel(volt_hbm, weight_hbm, held_ref, sems):
    copies = [
        pltpu.make_async_copy(volt_hbm.at[c], held_ref.at[c], sems.at[c])
        for c in range(held_ref.shape[0])
    ]
    for copy in copies:
        copy.start()
    for copy in copies:
        copy.wait()


def held_voltages(voltages, weights):
    return pl.pallas_call(
        hold_kernel,
        in_specs=[pl.BlockSpec(memory_space=pltpu.HBM), pl.BlockSpec(memory_space=pl.ANY)],
        out_specs=pl.BlockSpec(memory_space=pltpu.VMEM),
        scratch_shapes=[pltpu.SemaphoreType.DMA((voltages.shape[0],))],
        out_shape=pltpu.VMEM(voltages.shape, voltages.dtype),
        compiler_params=pltpu.CompilerParams(vmem_limit_bytes=VMEM_LIMIT),
    )(pltpu.with_memory_space_constraint(voltages, pltpu.HBM), weights)


def beam_kernel(first_turn, slab_ref, volt_ref, *refs):
    *weight_refs, out_ref, mixed = refs if first_turn == 0 else refs[1:]
    share, rows, _ = weight_refs[0].shape
    rows = rows * 2 // 3
    _, ports, _, samples = volt_ref.shape
    beams = out_ref.shape[1]
    step = pl.program_id(0)

    @pl.when(step == 0)
    def _():
        folded = [ref[c].astype(jnp.float32) for ref in weight_refs for c in range(share)]
        real_rows = stack(*[unfold(f) for f in folded])
        count, size = real_rows.shape
        row, _ = iotas(count, size)
        below, above = pltpu.roll(real_rows, count - 1, 0), pltpu.roll(real_rows, 1, 0)
        imag_rows = jnp.where(row % 2 == 0, -below, above)
        row, col = iotas(size, 2 * ports)
        to_even = (col == 2 * row).astype(jnp.float32).astype(jnp.bfloat16)
        to_odd = (col == 2 * row + 1).astype(jnp.float32).astype(jnp.bfloat16)
        placed = dot_nn(real_rows.astype(jnp.bfloat16), to_even)
        placed = (placed + dot_nn(imag_rows.astype(jnp.bfloat16), to_odd)).astype(jnp.bfloat16)
        for number in range(len(folded)):
            mixed[number] = placed[number * rows : (number + 1) * rows]

    first = (slab_ref[0] ^ (step + first_turn)) * share
    for c in range(share):
        volt = volt_ref[first + c].reshape(2 * ports, samples)
        formed = dot_nn(mixed[step * share + c], volt)
        out_ref[c] = formed[: 2 * beams].astype(jnp.bfloat16).reshape(beams, 2, samples)


def formed_beams(slab, voltages, weights, beams, formed=None):
    channels, ports, _, samples = voltages.shape
    share, rows, _ = weights[0].shape
    first_turn = 0 if formed is None else 1
    before = [] if formed is None else [formed]
    whole = pl.BlockSpec(weights[0].shape, lambda i, _: (0, 0, 0))
    return pl.pallas_call(
        functools.partial(beam_kernel, first_turn),
        grid_spec=pltpu.PrefetchScalarGridSpec(
            num_scalar_prefetch=1,
            grid=(len(weights),),
            in_specs=[pl.BlockSpec(memory_space=pltpu.VMEM)]
            + [pl.BlockSpec(memory_space=pl.ANY)] * len(before)
            + [whole] * len(weights),
            out_specs=pl.BlockSpec(
                (share, beams, 2, samples), lambda i, slab: (slab[0] ^ (i + first_turn), 0, 0, 0)
            ),
            scratch_shapes=[
                pltpu.VMEM((len(weights) * share, rows * 2 // 3, 2 * ports), jnp.bfloat16)
            ],
        ),
        out_shape=jax.ShapeDtypeStruct((channels, beams, 2, samples), jnp.bfloat16),
        input_output_aliases={} if formed is None else {2: 0},
        compiler_params=pltpu.CompilerParams(vmem_limit_bytes=VMEM_LIMIT),
    )(slab, voltages, *before, *weights)


def body(voltages, steering, beam_index, channel_flags):
    channel_count, _, port_count, _ = voltages.shape
    beam_count = beam_index.shape[0]
    slabs, blocks = lax.axis_size("slab"), lax.axis_size("chan")
    if channel_count != HW or slabs & (slabs - 1) or not LANES < port_count <= LANES * 3 // 2:
        raise ValueError("unsupported mesh")
    share = channel_count // slabs
    size = LANES + LANES // 2
    half = round_up(beam_count, 8)
    slab = lax.axis_index("slab").astype(jnp.int32).reshape(1)
    first_channel = (lax.axis_index("chan") * channel_count).astype(jnp.int32).reshape(1)
    chosen = chosen_vectors(slab, beam_index, steering, share, half, size)
    by_port = jnp.transpose(voltages, (0, 2, 1, 3))
    across, *inside, own = covariances(first_channel, channel_flags, by_port, size)
    pairs = [[(i, i + 1) for i in range(start, blocks - 1, 2)] for start in range(2)]
    inside_pairs, across_pairs = [ahead + [(j, i) for i, j in ahead] for ahead in pairs]
    across = lax.ppermute(across, "chan", across_pairs)
    inside = [lax.ppermute(part, "chan", inside_pairs) for part in inside]
    mine, *sent = windows(slab, own, across, *inside, slabs)

    def swap(arrays):
        return [
            lax.ppermute(array, "slab", [(i, i ^ turn) for i in range(slabs)])
            for turn, array in enumerate(arrays, 1)
        ]

    got = swap(sent)
    held = held_voltages(by_port, mine)
    first_share = first_channel + slab * share
    weights = solved_weights(first_share, channel_flags, held, mine, got, chosen, port_count, beam_count)
    others = swap([weights] * (slabs - 1))
    beams = formed_beams(slab, held, [weights], beam_count)
    beams = formed_beams(slab, held, others, beam_count, beams)
    return jnp.transpose(beams, (0, 2, 1, 3))


def solution(mesh):
    return jax.shard_map(
        body,
        mesh=mesh,
        in_specs=(P("chan", None, None, "slab"), P("chan", None, None, None), P(), P()),
        out_specs=P("chan", None, None, "slab"),
        check_vma=False,
    )
```

```python
import functools

import jax
import jax.numpy as jnp
from jax import lax
from jax.experimental import pallas as pl
from jax.experimental.pallas import tpu as pltpu
from jax.sharding import PartitionSpec as P

HW = 8


LOADING = 0.1

LANES = 128
VMEM_LIMIT = 24 * 1024 * 1024
SQUARINGS = 8


def round_up(value, multiple):
    return -(-value // multiple) * multiple


def dot_nn(left, right):
    return lax.dot_general(
        left, right, (((1,), (0,)), ((), ())), preferred_element_type=jnp.float32
    )


def dot_nt(left, right):
    return lax.dot_general(
        left, right, (((1,), (1,)), ((), ())), preferred_element_type=jnp.float32
    )


def iotas(rows, cols):
    return (
        lax.broadcasted_iota(jnp.int32, (rows, cols), 0),
        lax.broadcasted_iota(jnp.int32, (rows, cols), 1),
    )


def unfold(folded):
    size = folded.shape[0] * 2 // 3
    width = LANES // 2
    rest = jnp.concatenate([folded[size:, :width], folded[size:, width:]], axis=0)
    return jnp.concatenate([folded[:size], rest], axis=1)


def split(x):
    high = x.astype(jnp.bfloat16)
    return high, (x - high.astype(jnp.float32)).astype(jnp.bfloat16)


def combine(even_rows, odd_rows):
    lane = lax.broadcasted_iota(jnp.int32, even_rows.shape, 1)
    real = even_rows + pltpu.roll(odd_rows, LANES - 1, 1)
    return jnp.where(lane % 2 == 0, real, pltpu.roll(odd_rows, 1, 1) - even_rows)


def gram(volt, left_ref, right_ref):
    lead = left_ref.shape[1] // 2
    rest = volt.shape[0] - lead
    left, right = dot_nt(volt, volt[:lead]), dot_nt(volt[lead:], volt[lead:])
    left_ref[0, : volt.shape[0]] = left[:, :LANES]
    left_ref[1, : volt.shape[0], : lead - LANES] = left[:, LANES:]
    right_ref[0, :rest] = right[:, :LANES]
    right_ref[1, :rest, : rest - LANES] = right[:, LANES:]


def pack(left_ref, right_ref, out_ref):
    half = left_ref.shape[1] // 4

    def rows(ref, lanes, first, parity):
        return ref[lanes, pl.ds(2 * first + parity, half, stride=2), :]

    top = []
    for lanes in range(2):
        row, lane = iotas(half, LANES)
        gap = lane + lanes * LANES - 2 * row
        first = [rows(left_ref, lanes, 0, parity) for parity in range(2)]
        second = [rows(right_ref, lanes, 0, parity) for parity in range(2)]
        even = jnp.where(gap <= 0, first[0], jnp.where(gap == 1, -second[1], second[0]))
        odd = jnp.where(gap == 0, second[0], jnp.where(gap <= 1, first[1], second[1]))
        top.append((even, odd))
    low = [[rows(left_ref, lanes, half, parity) for parity in range(2)] for lanes in range(2)]
    width = LANES // 2
    side = [
        jnp.concatenate([above[:, :width], below[:, :width]], axis=1)
        for above, below in zip(top[1], low[1])
    ]
    for place, pair in enumerate((top[0], low[0], side)):
        out_ref[place * half : (place + 1) * half] = combine(*pair)


def covariance_kernel(
    first_ref,
    flags_hbm,
    volt_hbm,
    across_ref,
    inside_lead_ref,
    inside_rest_ref,
    own_ref,
    volts,
    lefts,
    rights,
    kept,
    flags_ref,
    sems,
    flags_sem,
):
    channels, ports, _, samples = volts.shape
    half = inside_lead_ref.shape[0]
    copies = [
        pltpu.make_async_copy(volt_hbm.at[c], volts.at[c], sems.at[c]) for c in range(channels)
    ]
    flags_copy = pltpu.make_async_copy(flags_hbm, flags_ref, flags_sem)
    flags_copy.start()
    groups = [range(c, c + 2) for c in range(0, channels, 2)]
    for group in groups[:2]:
        for c in group:
            copies[c].start()
    lefts[...] = jnp.zeros_like(lefts)
    rights[...] = jnp.zeros_like(rights)
    for number, group in enumerate(groups):
        for c in group:
            copies[c].wait()
        for later in groups[number + 2 : number + 3]:
            for c in later:
                copies[c].start()
        for c in group:
            gram(volts[c].reshape(2 * ports, samples), lefts.at[c % 4], rights.at[c % 4])
        for c in groups[number - 1] if number else ():
            pack(lefts.at[c % 4], rights.at[c % 4], kept.at[c])
    for c in groups[-1]:
        pack(lefts.at[c % 4], rights.at[c % 4], kept.at[c])
    flags_copy.wait()
    flags = [flags_ref[first_ref[0] + c].astype(jnp.float32) for c in range(channels)]
    odd_block = (first_ref[0] // channels) % 2 == 1
    for start in range(0, kept.shape[1], 16):
        part = slice(start, start + 16)
        plain = [kept[c, part] for c in range(channels)]
        masked = [plain[c] * flags[c] for c in range(channels)]
        up_to, onward = [masked[0]], [masked[-1]]
        for c in range(1, channels):
            up_to.append(up_to[-1] + masked[c])
            onward.append(onward[-1] + masked[channels - 1 - c])
        for c in range(channels):
            up, down = onward[channels - 1 - c], up_to[c]
            across_ref[c, part] = jnp.where(odd_block, up, down).astype(across_ref.dtype)
            inside = jnp.where(odd_block, down, up).astype(across_ref.dtype)
            if c < half:
                inside_lead_ref[c, part] = inside
            else:
                inside_rest_ref[c - half, part] = inside
            own_ref[c, part] = up_to[-1] + (1.0 - flags[c]) * plain[c]


def covariances(first, flags, voltages, size):
    channels, ports, _, samples = voltages.shape
    folded = (channels, size + size // 2, LANES)
    half = channels // 2
    smem = pl.BlockSpec(memory_space=pltpu.SMEM)
    vmem = pl.BlockSpec(memory_space=pltpu.VMEM)
    return pl.pallas_call(
        covariance_kernel,
        in_specs=[smem] + [pl.BlockSpec(memory_space=pltpu.HBM)] * 2,
        out_specs=[vmem] * 4,
        scratch_shapes=[
            pltpu.VMEM(voltages.shape, voltages.dtype),
            pltpu.VMEM((4, 2, 2 * size, LANES), jnp.float32),
            pltpu.VMEM((4, 2, size, LANES), jnp.float32),
            pltpu.VMEM(folded, jnp.float32),
            pltpu.SMEM(flags.shape, flags.dtype),
            pltpu.SemaphoreType.DMA((channels,)),
            pltpu.SemaphoreType.DMA,
        ],
        out_shape=[
            pltpu.VMEM(folded, jnp.bfloat16),
            pltpu.VMEM((half, *folded[1:]), jnp.bfloat16),
            pltpu.VMEM((channels - half, *folded[1:]), jnp.bfloat16),
            pltpu.VMEM(folded, jnp.float32),
        ],
        compiler_params=pltpu.CompilerParams(vmem_limit_bytes=VMEM_LIMIT),
    )(first, *[pltpu.with_memory_space_constraint(a, pltpu.HBM) for a in (flags, voltages)])


def window_kernel(slab_ref, own_ref, inside_ref, across_ref, mine_ref, *sent_refs):
    share = mine_ref.shape[0]

    def window(slab):
        rows = pl.ds(slab * share, share)
        ends = inside_ref[rows].astype(jnp.float32) + across_ref[rows].astype(jnp.float32)
        return own_ref[rows] + ends

    mine_ref[...] = window(slab_ref[0])
    for turn, sent_ref in enumerate(sent_refs, 1):
        sent_ref[...] = window(slab_ref[0] ^ turn).astype(sent_ref.dtype)


def windows(slab, own, inside, across, slabs):
    shape = (own.shape[0] // slabs,) + own.shape[1:]
    return pl.pallas_call(
        window_kernel,
        in_specs=[pl.BlockSpec(memory_space=pltpu.SMEM)]
        + [pl.BlockSpec(own.shape, lambda: (0, 0, 0))] * 3,
        out_specs=[pl.BlockSpec(shape, lambda: (0, 0, 0))] * slabs,
        out_shape=[jax.ShapeDtypeStruct(shape, jnp.float32)]
        + [jax.ShapeDtypeStruct(shape, jnp.bfloat16)] * (slabs - 1),
        compiler_params=pltpu.CompilerParams(vmem_limit_bytes=VMEM_LIMIT),
    )(slab, own, inside, across)


def choose_kernel(slab_ref, index_ref, steer_ref, out_ref):
    beams, half = index_ref.shape[0], out_ref.shape[1] // 2
    ports = steer_ref.shape[3]
    out_ref[...] = jnp.zeros_like(out_ref)
    for channel in range(out_ref.shape[0]):
        for part in range(2):
            for beam in range(beams):
                row = steer_ref[channel, part, pl.ds(index_ref[beam], 1), :]
                out_ref[channel, pl.ds(part * half + beam, 1), pl.ds(0, ports)] = row


def chosen_vectors(slab, beam_index, steering, share, half, size):
    directions, ports = steering.shape[2:]
    return pl.pallas_call(
        choose_kernel,
        grid_spec=pltpu.PrefetchScalarGridSpec(
            num_scalar_prefetch=2,
            grid=(1,),
            in_specs=[
                pl.BlockSpec((share, 2, directions, ports), lambda i, slab, _: (slab[0], 0, 0, 0))
            ],
            out_specs=pl.BlockSpec((share, 2 * half, size), lambda i, *_: (0, 0, 0)),
        ),
        out_shape=jax.ShapeDtypeStruct((share, 2 * half, size), jnp.float32),
        compiler_params=pltpu.CompilerParams(vmem_limit_bytes=VMEM_LIMIT),
    )(slab, beam_index, steering)


def unpack(folded):
    packed = unfold(folded)
    size = packed.shape[0]
    half = size // 2
    row, col = iotas(size, 2 * LANES)
    spread = (row == jnp.where(col < LANES, 2 * col, 2 * (col - LANES) + 1)) & (col % LANES < half)
    spread = spread.astype(jnp.float32).astype(jnp.bfloat16)
    high, rest = split(packed)
    lowest = packed - high.astype(jnp.float32) - rest.astype(jnp.float32)
    parts = dot_nn(jnp.concatenate([high, rest, lowest.astype(jnp.bfloat16)], axis=0), spread)
    parts = parts[:size] + (parts[size : 2 * size] + parts[2 * size :])
    real, imag = parts[:, :half], parts[:, LANES : LANES + half]
    row, col = iotas(half, half)
    turned_real, turned_imag = real[:half].T, imag[:half].T
    first_real = jnp.where(row >= col, real[:half], turned_real)
    first_imag = jnp.where(row > col, imag[:half], jnp.where(row < col, -turned_imag, 0.0))
    second_real = jnp.where(row < col, real[:half], jnp.where(row > col, turned_real, imag[:half]))
    second_imag = jnp.where(row < col, imag[:half], jnp.where(row > col, -turned_imag, 0.0))

    def blocks(first, second, low, high):
        return jnp.concatenate(
            [jnp.concatenate([first, high], axis=1), jnp.concatenate([low, second], axis=1)], axis=0
        )

    low_real, low_imag = real[half:], imag[half:]
    return (
        blocks(first_real, second_real, low_real, low_real.T),
        blocks(first_imag, second_imag, low_imag, -low_imag.T),
    )


def gains(bound, steps):
    spread, out = (bound - 1.0) / (bound + 1.0), []
    for _ in range(steps):
        centre = spread * spread / 2
        out.append((spread, 1.0 / (1.0 - centre)))
        spread = centre / (1.0 - centre)
    return out


def stack(*arrays):
    return jnp.concatenate(arrays, axis=0)


def multiply(y, real, imag, squares=True):
    n, m = y.shape[0], real.shape[0]
    half = n // 2
    (rh, rl), (ih, il), (yh, yl) = split(real), split(imag), split(y)
    if squares:
        by_rh, by_rl = dot_nn(stack(yh, yl, rh), rh), dot_nn(stack(yh, rh), rl)
        by_ih, by_il = dot_nn(stack(yh, yl, ih), ih), dot_nn(yh, il)
    else:
        by_rh, by_rl = dot_nn(stack(yh, yl), rh), dot_nn(yh, rl)
        by_ih, by_il = dot_nn(stack(yh, yl), ih), dot_nn(yh, il)
    with_real = by_rh[:n] + by_rh[n : 2 * n] + by_rl[:n]
    with_imag = by_ih[:n] + by_ih[n : 2 * n] + by_il
    product = stack(with_real[:half] + with_imag[half:], with_real[half:] - with_imag[:half])
    if not squares:
        return product, None, None
    cross = dot_nn(stack(rh, rl), ih)
    mixed = by_rl[n:] - dot_nn(ih, il)
    rr_less_ii = by_rh[2 * n :] - by_ih[2 * n :] + (mixed + mixed.T)
    ri = cross[:m] + cross[m:] + dot_nn(rh, il)
    return product, rr_less_ii, ri - ri.T


def multiply_once(y, real, imag, squares):
    n, m = y.shape[0], real.shape[0]
    half = n // 2
    rh, ih, yh = (a.astype(jnp.bfloat16) for a in (real, imag, y))
    by_rh = dot_nn(stack(yh, rh) if squares else yh, rh)
    by_ih = dot_nn(stack(yh, ih, rh) if squares else yh, ih)
    product = stack(by_rh[:half] + by_ih[half:n], by_rh[half:n] - by_ih[:half])
    if not squares:
        return product, None, None
    ri = by_ih[n + m :]
    return product, by_rh[n:] - by_ih[n : n + m], ri - ri.T


def solve_kernel(ports, beams, first_ref, flags_ref, held_ref, *refs):
    own_ref, *got_refs, chosen_ref, weight_ref = refs
    share, half, size = weight_ref.shape[0], chosen_ref.shape[1] // 2, chosen_ref.shape[2]
    bound = ports / LOADING + 1.0
    row, col = iotas(size, size)
    identity = jnp.where(row == col, 1.0, 0.0)
    channels = range(share)
    state = []
    for c in channels:
        folded = own_ref[c]
        for got_ref in got_refs:
            folded = folded + got_ref[c].astype(jnp.float32)
        real, imag = unpack(folded)
        trace = jnp.sum(jnp.sum(real * identity, axis=0, keepdims=True), axis=1, keepdims=True)
        loading = trace * (LOADING / ports)
        scale = 2.0 / (loading * (1.0 + bound))
        real = real + jnp.where((row == col) & (row < ports), loading, 0.0)
        state.append((real * scale, imag * scale, chosen_ref[c] * scale))
    steps = gains(bound, SQUARINGS)
    for number, (spread, gain) in enumerate(steps):
        squares = number + 1 < len(steps)
        for c in channels:
            real, imag, y = state[c]
            if number == len(steps) - 2:
                real, imag = identity - real, -imag
            if number < len(steps) - 2:
                product, real2, imag2 = multiply(y, real, imag)
                y = gain * (2.0 * y - product)
                real, imag = gain * (2.0 * real - real2), gain * (2.0 * imag - imag2)
            elif squares:
                product, _, _ = multiply(y, real, imag, squares=False)
                _, real, imag = multiply_once(y, real, imag, True)
                y = gain * (y + product)
                real, imag = gain * (real - identity * (spread * spread / 2)), gain * imag
            else:
                y = gain * (y + multiply_once(y, real, imag, False)[0])
            state[c] = real, imag, y
    beam = lax.broadcasted_iota(jnp.int32, (half, 1), 0)
    row, col = iotas(2 * half, 2 * half)
    place = jnp.where(row % 2 == 0, row // 2, row // 2 + half)
    order = jnp.where(col == place, jnp.where(row % 2 == 0, 1.0, -1.0), 0.0).astype(jnp.bfloat16)
    for c in channels:
        y = state[c][2]
        sums = jnp.sum(y * chosen_ref[c], axis=1, keepdims=True)
        denominator = jnp.where(beam < beams, sums[:half] + sums[half:], 1.0)
        flag = flags_ref[first_ref[0] + c].astype(jnp.float32)
        factor = jnp.where(beam < beams, flag / denominator, 0.0)
        weights = dot_nn(order, (y * stack(factor, factor)).astype(jnp.bfloat16))
        high = weights[:, LANES:]
        weight_ref[c, : 2 * half] = weights[:, :LANES].astype(jnp.bfloat16)
        weight_ref[c, 2 * half :] = jnp.concatenate([high[:half], high[half:]], axis=1).astype(
            jnp.bfloat16
        )


def solved_weights(first, flags, held, own, got, chosen, ports, beams):
    share, rows, _ = chosen.shape
    smem = pl.BlockSpec(memory_space=pltpu.SMEM)
    whole = [pl.BlockSpec(a.shape, lambda: (0, 0, 0)) for a in (own, *got, chosen)]
    shape = (share, rows + rows // 2, LANES)
    return pl.pallas_call(
        functools.partial(solve_kernel, ports, beams),
        in_specs=[smem, smem, pl.BlockSpec(memory_space=pl.ANY)] + whole,
        out_specs=pl.BlockSpec(shape, lambda: (0, 0, 0)),
        out_shape=jax.ShapeDtypeStruct(shape, jnp.bfloat16),
        compiler_params=pltpu.CompilerParams(vmem_limit_bytes=VMEM_LIMIT),
    )(first, flags, held, own, *got, chosen)


def hold_kernel(volt_hbm, weight_hbm, held_ref, sems):
    copies = [
        pltpu.make_async_copy(volt_hbm.at[c], held_ref.at[c], sems.at[c])
        for c in range(held_ref.shape[0])
    ]
    for copy in copies:
        copy.start()
    for copy in copies:
        copy.wait()


def held_voltages(voltages, weights):
    return pl.pallas_call(
        hold_kernel,
        in_specs=[pl.BlockSpec(memory_space=pltpu.HBM), pl.BlockSpec(memory_space=pl.ANY)],
        out_specs=pl.BlockSpec(memory_space=pltpu.VMEM),
        scratch_shapes=[pltpu.SemaphoreType.DMA((voltages.shape[0],))],
        out_shape=pltpu.VMEM(voltages.shape, voltages.dtype),
        compiler_params=pltpu.CompilerParams(vmem_limit_bytes=VMEM_LIMIT),
    )(pltpu.with_memory_space_constraint(voltages, pltpu.HBM), weights)


def beam_kernel(first_turn, slab_ref, volt_ref, *refs):
    *weight_refs, out_ref, mixed = refs if first_turn == 0 else refs[1:]
    share, rows, _ = weight_refs[0].shape
    rows = rows * 2 // 3
    _, ports, _, samples = volt_ref.shape
    beams = out_ref.shape[1]
    step = pl.program_id(0)

    @pl.when(step == 0)
    def _():
        folded = [ref[c].astype(jnp.float32) for ref in weight_refs for c in range(share)]
        real_rows = stack(*[unfold(f) for f in folded])
        count, size = real_rows.shape
        row, _ = iotas(count, size)
        below, above = pltpu.roll(real_rows, count - 1, 0), pltpu.roll(real_rows, 1, 0)
        imag_rows = jnp.where(row % 2 == 0, -below, above)
        row, col = iotas(size, 2 * ports)
        to_even = (col == 2 * row).astype(jnp.float32).astype(jnp.bfloat16)
        to_odd = (col == 2 * row + 1).astype(jnp.float32).astype(jnp.bfloat16)
        placed = dot_nn(real_rows.astype(jnp.bfloat16), to_even)
        placed = (placed + dot_nn(imag_rows.astype(jnp.bfloat16), to_odd)).astype(jnp.bfloat16)
        for number in range(len(folded)):
            mixed[number] = placed[number * rows : (number + 1) * rows]

    first = (slab_ref[0] ^ (step + first_turn)) * share
    for c in range(share):
        volt = volt_ref[first + c].reshape(2 * ports, samples)
        formed = dot_nn(mixed[step * share + c], volt)
        out_ref[c] = formed[: 2 * beams].astype(jnp.bfloat16).reshape(beams, 2, samples)


def formed_beams(slab, voltages, weights, beams, first_turn=0, formed=None):
    channels, ports, _, samples = voltages.shape
    share, rows, _ = weights[0].shape
    before = [] if formed is None else [formed]
    whole = pl.BlockSpec(weights[0].shape, lambda i, _: (0, 0, 0))
    return pl.pallas_call(
        functools.partial(beam_kernel, first_turn),
        grid_spec=pltpu.PrefetchScalarGridSpec(
            num_scalar_prefetch=1,
            grid=(len(weights),),
            in_specs=[pl.BlockSpec(memory_space=pltpu.VMEM)]
            + [pl.BlockSpec(memory_space=pl.ANY)] * len(before)
            + [whole] * len(weights),
            out_specs=pl.BlockSpec(
                (share, beams, 2, samples), lambda i, slab: (slab[0] ^ (i + first_turn), 0, 0, 0)
            ),
            scratch_shapes=[
                pltpu.VMEM((len(weights) * share, rows * 2 // 3, 2 * ports), jnp.bfloat16)
            ],
        ),
        out_shape=jax.ShapeDtypeStruct((channels, beams, 2, samples), jnp.bfloat16),
        input_output_aliases={} if formed is None else {2: 0},
        compiler_params=pltpu.CompilerParams(vmem_limit_bytes=VMEM_LIMIT),
    )(slab, voltages, *before, *weights)


def body(voltages, steering, beam_index, channel_flags):
    channel_count, _, port_count, _ = voltages.shape
    beam_count = beam_index.shape[0]
    slabs, blocks = lax.axis_size("slab"), lax.axis_size("chan")
    if channel_count != HW or slabs & (slabs - 1) or not LANES < port_count <= LANES * 3 // 2:
        raise ValueError("unsupported mesh")
    share = channel_count // slabs
    size = LANES + LANES // 2
    half = round_up(beam_count, 8)
    slab = lax.axis_index("slab").astype(jnp.int32).reshape(1)
    first_channel = (lax.axis_index("chan") * channel_count).astype(jnp.int32).reshape(1)
    chosen = chosen_vectors(slab, beam_index, steering, share, half, size)
    by_port = jnp.transpose(voltages, (0, 2, 1, 3))
    across, *inside, own = covariances(first_channel, channel_flags, by_port, size)
    pairs = [[(i, i + 1) for i in range(start, blocks - 1, 2)] for start in range(2)]
    inside_pairs, across_pairs = [ahead + [(j, i) for i, j in ahead] for ahead in pairs]
    across = lax.ppermute(across, "chan", across_pairs)
    inside = jnp.concatenate([lax.ppermute(part, "chan", inside_pairs) for part in inside], axis=0)
    mine, *sent = windows(slab, own, inside, across, slabs)

    def swap(arrays):
        return [
            lax.ppermute(array, "slab", [(i, i ^ turn) for i in range(slabs)])
            for turn, array in enumerate(arrays, 1)
        ]

    got = swap(sent)
    held = held_voltages(by_port, mine)
    first_share = first_channel + slab * share
    weights = solved_weights(first_share, channel_flags, held, mine, got, chosen, port_count, beam_count)
    others = swap([weights] * (slabs - 1))
    beams = formed_beams(slab, held, [weights], beam_count)
    beams = formed_beams(slab, held, others[-1:], beam_count, slabs - 1, beams)
    beams = formed_beams(slab, held, others[:-1], beam_count, 1, beams)
    return jnp.transpose(beams, (0, 2, 1, 3))


def solution(mesh):
    return jax.shard_map(
        body,
        mesh=mesh,
        in_specs=(P("chan", None, None, "slab"), P("chan", None, None, None), P(), P()),
        out_specs=P("chan", None, None, "slab"),
        check_vma=False,
    )
```

```python
import functools

import jax
import jax.numpy as jnp
from jax import lax
from jax.experimental import pallas as pl
from jax.experimental.pallas import tpu as pltpu
from jax.sharding import PartitionSpec as P

HW = 8


LOADING = 0.1

LANES = 128
VMEM_LIMIT = 24 * 1024 * 1024
SQUARINGS = 8


def round_up(value, multiple):
    return -(-value // multiple) * multiple


def dot_nn(left, right):
    return lax.dot_general(
        left, right, (((1,), (0,)), ((), ())), preferred_element_type=jnp.float32
    )


def dot_nt(left, right):
    return lax.dot_general(
        left, right, (((1,), (1,)), ((), ())), preferred_element_type=jnp.float32
    )


def iotas(rows, cols):
    return (
        lax.broadcasted_iota(jnp.int32, (rows, cols), 0),
        lax.broadcasted_iota(jnp.int32, (rows, cols), 1),
    )


def unfold(folded, size):
    width = LANES // 2
    rest = folded[size : size + size // 2]
    rest = jnp.concatenate([rest[:, :width], rest[:, width:]], axis=0)
    return jnp.concatenate([folded[:size], rest], axis=1)


def split(x):
    high = x.astype(jnp.bfloat16)
    return high, (x - high.astype(jnp.float32)).astype(jnp.bfloat16)


def combine(even_rows, odd_rows):
    lane = lax.broadcasted_iota(jnp.int32, even_rows.shape, 1)
    real = even_rows + pltpu.roll(odd_rows, LANES - 1, 1)
    return jnp.where(lane % 2 == 0, real, pltpu.roll(odd_rows, 1, 1) - even_rows)


def gram(volt, left_ref, right_ref):
    lead = round_up(volt.shape[0], 16) // 2
    rest = volt.shape[0] - lead
    left, right = dot_nt(volt, volt[:lead]), dot_nt(volt[lead:], volt[lead:])
    left_ref[0, : volt.shape[0]] = left[:, :LANES]
    left_ref[1, : volt.shape[0], : lead - LANES] = left[:, LANES:]
    right_ref[0, :rest] = right[:, :LANES]
    right_ref[1, :rest, : rest - LANES] = right[:, LANES:]


def pack(left_ref, right_ref, out_ref):
    half = out_ref.shape[0] // 3

    def rows(ref, lanes, first, parity):
        return ref[lanes, pl.ds(2 * first + parity, half, stride=2), :]

    top = []
    for lanes in range(2):
        row, lane = iotas(half, LANES)
        gap = lane + lanes * LANES - 2 * row
        first = [rows(left_ref, lanes, 0, parity) for parity in range(2)]
        second = [rows(right_ref, lanes, 0, parity) for parity in range(2)]
        even = jnp.where(gap <= 0, first[0], jnp.where(gap == 1, -second[1], second[0]))
        odd = jnp.where(gap == 0, second[0], jnp.where(gap <= 1, first[1], second[1]))
        top.append((even, odd))
    low = [[rows(left_ref, lanes, half, parity) for parity in range(2)] for lanes in range(2)]
    width = LANES // 2
    side = [
        jnp.concatenate([above[:, :width], below[:, :width]], axis=1)
        for above, below in zip(top[1], low[1])
    ]
    for place, pair in enumerate((top[0], low[0], side)):
        out_ref[place * half : (place + 1) * half] = combine(*pair)


def covariance_kernel(
    first_ref,
    flags_hbm,
    volt_hbm,
    across_ref,
    inside_lead_ref,
    inside_rest_ref,
    own_ref,
    volts,
    lefts,
    rights,
    kept,
    flags_ref,
    sems,
    flags_sem,
):
    channels, ports, _, samples = volts.shape
    half = inside_lead_ref.shape[0]
    copies = [
        pltpu.make_async_copy(volt_hbm.at[c], volts.at[c], sems.at[c]) for c in range(channels)
    ]
    flags_copy = pltpu.make_async_copy(flags_hbm, flags_ref, flags_sem)
    flags_copy.start()
    groups = [range(c, c + 2) for c in range(0, channels, 2)]
    for group in groups[:2]:
        for c in group:
            copies[c].start()
    lefts[...] = jnp.zeros_like(lefts)
    rights[...] = jnp.zeros_like(rights)
    for number, group in enumerate(groups):
        for c in group:
            copies[c].wait()
        for later in groups[number + 2 : number + 3]:
            for c in later:
                copies[c].start()
        for c in group:
            gram(volts[c].reshape(2 * ports, samples), lefts.at[c % 4], rights.at[c % 4])
        for c in groups[number - 1] if number else ():
            pack(lefts.at[c % 4], rights.at[c % 4], kept.at[c])
    for c in groups[-1]:
        pack(lefts.at[c % 4], rights.at[c % 4], kept.at[c])
    flags_copy.wait()
    flags = [flags_ref[first_ref[0] + c].astype(jnp.float32) for c in range(channels)]
    odd_block = (first_ref[0] // channels) % 2 == 1
    for start in range(0, kept.shape[1], 16):
        part = slice(start, start + 16)
        plain = [kept[c, part] for c in range(channels)]
        masked = [plain[c] * flags[c] for c in range(channels)]
        up_to, onward = [masked[0]], [masked[-1]]
        for c in range(1, channels):
            up_to.append(up_to[-1] + masked[c])
            onward.append(onward[-1] + masked[channels - 1 - c])
        for c in range(channels):
            up, down = onward[channels - 1 - c], up_to[c]
            across_ref[c, part] = jnp.where(odd_block, up, down).astype(across_ref.dtype)
            inside = jnp.where(odd_block, down, up).astype(across_ref.dtype)
            if c < half:
                inside_lead_ref[c, part] = inside
            else:
                inside_rest_ref[c - half, part] = inside
            own_ref[c, part] = up_to[-1] + (1.0 - flags[c]) * plain[c]


def covariances(first, flags, voltages, size):
    channels, ports, _, samples = voltages.shape
    folded = (channels, size + size // 2, LANES)
    half = channels // 2
    smem = pl.BlockSpec(memory_space=pltpu.SMEM)
    vmem = pl.BlockSpec(memory_space=pltpu.VMEM)
    return pl.pallas_call(
        covariance_kernel,
        in_specs=[smem] + [pl.BlockSpec(memory_space=pltpu.HBM)] * 2,
        out_specs=[vmem] * 4,
        scratch_shapes=[
            pltpu.VMEM(voltages.shape, voltages.dtype),
            pltpu.VMEM((4, 2, 2 * size + 8, LANES), jnp.float32),
            pltpu.VMEM((4, 2, size + 8, LANES), jnp.float32),
            pltpu.VMEM(folded, jnp.float32),
            pltpu.SMEM(flags.shape, flags.dtype),
            pltpu.SemaphoreType.DMA((channels,)),
            pltpu.SemaphoreType.DMA,
        ],
        out_shape=[
            pltpu.VMEM(folded, jnp.bfloat16),
            pltpu.VMEM((half, *folded[1:]), jnp.bfloat16),
            pltpu.VMEM((channels - half, *folded[1:]), jnp.bfloat16),
            pltpu.VMEM(folded, jnp.float32),
        ],
        compiler_params=pltpu.CompilerParams(vmem_limit_bytes=VMEM_LIMIT),
    )(first, *[pltpu.with_memory_space_constraint(a, pltpu.HBM) for a in (flags, voltages)])


def window_kernel(slab_ref, own_ref, inside_ref, across_ref, mine_ref, *sent_refs):
    share = mine_ref.shape[0]

    def window(slab):
        rows = pl.ds(slab * share, share)
        ends = inside_ref[rows].astype(jnp.float32) + across_ref[rows].astype(jnp.float32)
        return own_ref[rows] + ends

    mine_ref[...] = window(slab_ref[0])
    for turn, sent_ref in enumerate(sent_refs, 1):
        sent_ref[...] = window(slab_ref[0] ^ turn).astype(sent_ref.dtype)


def windows(slab, own, inside, across, slabs):
    shape = (own.shape[0] // slabs,) + own.shape[1:]
    return pl.pallas_call(
        window_kernel,
        in_specs=[pl.BlockSpec(memory_space=pltpu.SMEM)]
        + [pl.BlockSpec(own.shape, lambda: (0, 0, 0))] * 3,
        out_specs=[pl.BlockSpec(shape, lambda: (0, 0, 0))] * slabs,
        out_shape=[jax.ShapeDtypeStruct(shape, jnp.float32)]
        + [jax.ShapeDtypeStruct(shape, jnp.bfloat16)] * (slabs - 1),
        compiler_params=pltpu.CompilerParams(vmem_limit_bytes=VMEM_LIMIT),
    )(slab, own, inside, across)


def choose_kernel(slab_ref, index_ref, steer_ref, out_ref):
    beams, half = index_ref.shape[0], out_ref.shape[1] // 2
    ports = steer_ref.shape[3]
    out_ref[...] = jnp.zeros_like(out_ref)
    for channel in range(out_ref.shape[0]):
        for part in range(2):
            for beam in range(beams):
                row = steer_ref[channel, part, pl.ds(index_ref[beam], 1), :]
                out_ref[channel, pl.ds(part * half + beam, 1), pl.ds(0, ports)] = row


def chosen_vectors(slab, beam_index, steering, share, half, size):
    directions, ports = steering.shape[2:]
    return pl.pallas_call(
        choose_kernel,
        grid_spec=pltpu.PrefetchScalarGridSpec(
            num_scalar_prefetch=2,
            grid=(1,),
            in_specs=[
                pl.BlockSpec((share, 2, directions, ports), lambda i, slab, _: (slab[0], 0, 0, 0))
            ],
            out_specs=pl.BlockSpec((share, 2 * half, size), lambda i, *_: (0, 0, 0)),
        ),
        out_shape=jax.ShapeDtypeStruct((share, 2 * half, size), jnp.float32),
        compiler_params=pltpu.CompilerParams(vmem_limit_bytes=VMEM_LIMIT),
    )(slab, beam_index, steering)


def unpack(folded):
    size = folded.shape[0] * 2 // 3
    packed = unfold(folded, size)
    half = size // 2
    row, col = iotas(size, 2 * LANES)
    spread = (row == jnp.where(col < LANES, 2 * col, 2 * (col - LANES) + 1)) & (col % LANES < half)
    spread = spread.astype(jnp.float32).astype(jnp.bfloat16)
    high, rest = split(packed)
    lowest = packed - high.astype(jnp.float32) - rest.astype(jnp.float32)
    parts = dot_nn(jnp.concatenate([high, rest, lowest.astype(jnp.bfloat16)], axis=0), spread)
    parts = parts[:size] + (parts[size : 2 * size] + parts[2 * size :])
    real, imag = parts[:, :half], parts[:, LANES : LANES + half]
    row, col = iotas(half, half)
    turned_real, turned_imag = real[:half].T, imag[:half].T
    first_real = jnp.where(row >= col, real[:half], turned_real)
    first_imag = jnp.where(row > col, imag[:half], jnp.where(row < col, -turned_imag, 0.0))
    second_real = jnp.where(row < col, real[:half], jnp.where(row > col, turned_real, imag[:half]))
    second_imag = jnp.where(row < col, imag[:half], jnp.where(row > col, -turned_imag, 0.0))

    def blocks(first, second, low, high):
        return jnp.concatenate(
            [jnp.concatenate([first, high], axis=1), jnp.concatenate([low, second], axis=1)], axis=0
        )

    low_real, low_imag = real[half:], imag[half:]
    return (
        blocks(first_real, second_real, low_real, low_real.T),
        blocks(first_imag, second_imag, low_imag, -low_imag.T),
    )


def gains(bound, steps):
    spread, out = (bound - 1.0) / (bound + 1.0), []
    for _ in range(steps):
        centre = spread * spread / 2
        out.append((spread, 1.0 / (1.0 - centre)))
        spread = centre / (1.0 - centre)
    return out


def stack(*arrays):
    return jnp.concatenate(arrays, axis=0)


def multiply(y, real, imag, squares=True):
    n, m = y.shape[0], real.shape[0]
    half = n // 2
    (rh, rl), (ih, il), (yh, yl) = split(real), split(imag), split(y)
    if squares:
        by_rh, by_rl = dot_nn(stack(yh, yl, rh), rh), dot_nn(stack(yh, rh), rl)
        by_ih, by_il = dot_nn(stack(yh, yl, ih), ih), dot_nn(yh, il)
    else:
        by_rh, by_rl = dot_nn(stack(yh, yl), rh), dot_nn(yh, rl)
        by_ih, by_il = dot_nn(stack(yh, yl), ih), dot_nn(yh, il)
    with_real = by_rh[:n] + by_rh[n : 2 * n] + by_rl[:n]
    with_imag = by_ih[:n] + by_ih[n : 2 * n] + by_il
    product = stack(with_real[:half] + with_imag[half:], with_real[half:] - with_imag[:half])
    if not squares:
        return product, None, None
    cross = dot_nn(stack(rh, rl), ih)
    mixed = by_rl[n:] - dot_nn(ih, il)
    rr_less_ii = by_rh[2 * n :] - by_ih[2 * n :] + (mixed + mixed.T)
    ri = cross[:m] + cross[m:] + dot_nn(rh, il)
    return product, rr_less_ii, ri - ri.T


def multiply_once(y, real, imag, squares):
    n, m = y.shape[0], real.shape[0]
    half = n // 2
    rh, ih, yh = (a.astype(jnp.bfloat16) for a in (real, imag, y))
    by_rh = dot_nn(stack(yh, rh) if squares else yh, rh)
    by_ih = dot_nn(stack(yh, ih, rh) if squares else yh, ih)
    product = stack(by_rh[:half] + by_ih[half:n], by_rh[half:n] - by_ih[:half])
    if not squares:
        return product, None, None
    ri = by_ih[n + m :]
    return product, by_rh[n:] - by_ih[n : n + m], ri - ri.T


def solve_kernel(ports, beams, first_ref, flags_ref, held_ref, *refs):
    own_ref, *got_refs, chosen_ref, weight_ref = refs
    share, half, size = weight_ref.shape[0], chosen_ref.shape[1] // 2, chosen_ref.shape[2]
    bound = ports / LOADING + 1.0
    row, col = iotas(size, size)
    identity = jnp.where(row == col, 1.0, 0.0)
    channels = range(share)
    state = []
    for c in channels:
        folded = own_ref[c]
        for got_ref in got_refs:
            folded = folded + got_ref[c].astype(jnp.float32)
        real, imag = unpack(folded)
        trace = jnp.sum(jnp.sum(real * identity, axis=0, keepdims=True), axis=1, keepdims=True)
        loading = trace * (LOADING / ports)
        scale = 2.0 / (loading * (1.0 + bound))
        real = real + jnp.where((row == col) & (row < ports), loading, 0.0)
        state.append((real * scale, imag * scale, chosen_ref[c] * scale))
    steps = gains(bound, SQUARINGS)
    for number, (spread, gain) in enumerate(steps):
        squares = number + 1 < len(steps)
        for c in channels:
            real, imag, y = state[c]
            if number == len(steps) - 2:
                real, imag = identity - real, -imag
            if number < len(steps) - 2:
                product, real2, imag2 = multiply(y, real, imag)
                y = gain * (2.0 * y - product)
                real, imag = gain * (2.0 * real - real2), gain * (2.0 * imag - imag2)
            elif squares:
                product, _, _ = multiply(y, real, imag, squares=False)
                _, real, imag = multiply_once(y, real, imag, True)
                y = gain * (y + product)
                real, imag = gain * (real - identity * (spread * spread / 2)), gain * imag
            else:
                y = gain * (y + multiply_once(y, real, imag, False)[0])
            state[c] = real, imag, y
    beam = lax.broadcasted_iota(jnp.int32, (half, 1), 0)
    row, col = iotas(2 * half, 2 * half)
    place = jnp.where(row % 2 == 0, row // 2, row // 2 + half)
    order = jnp.where(col == place, jnp.where(row % 2 == 0, 1.0, -1.0), 0.0).astype(jnp.bfloat16)
    for c in channels:
        y = state[c][2]
        sums = jnp.sum(y * chosen_ref[c], axis=1, keepdims=True)
        denominator = jnp.where(beam < beams, sums[:half] + sums[half:], 1.0)
        flag = flags_ref[first_ref[0] + c].astype(jnp.float32)
        factor = jnp.where(beam < beams, flag / denominator, 0.0)
        weights = dot_nn(order, (y * stack(factor, factor)).astype(jnp.bfloat16))
        high = weights[:, LANES:]
        weight_ref[c, : 2 * half] = weights[:, :LANES].astype(jnp.bfloat16)
        high = jnp.concatenate([high[:half], high[half:]], axis=1)
        spare = weight_ref.shape[1] - 3 * half
        if spare:
            high = stack(high, jnp.zeros((spare, LANES), jnp.float32))
        weight_ref[c, 2 * half :] = high.astype(jnp.bfloat16)


def solved_weights(first, flags, held, own, got, chosen, ports, beams):
    share, rows, _ = chosen.shape
    smem = pl.BlockSpec(memory_space=pltpu.SMEM)
    whole = [pl.BlockSpec(a.shape, lambda: (0, 0, 0)) for a in (own, *got, chosen)]
    shape = (share, round_up(rows + rows // 2, 16), LANES)
    return pl.pallas_call(
        functools.partial(solve_kernel, ports, beams),
        in_specs=[smem, smem, pl.BlockSpec(memory_space=pl.ANY)] + whole,
        out_specs=pl.BlockSpec(shape, lambda: (0, 0, 0)),
        out_shape=jax.ShapeDtypeStruct(shape, jnp.bfloat16),
        compiler_params=pltpu.CompilerParams(vmem_limit_bytes=VMEM_LIMIT),
    )(first, flags, held, own, *got, chosen)


def hold_kernel(volt_hbm, weight_hbm, held_ref, sems):
    copies = [
        pltpu.make_async_copy(volt_hbm.at[c], held_ref.at[c], sems.at[c])
        for c in range(held_ref.shape[0])
    ]
    for copy in copies:
        copy.start()
    for copy in copies:
        copy.wait()


def held_voltages(voltages, weights):
    return pl.pallas_call(
        hold_kernel,
        in_specs=[pl.BlockSpec(memory_space=pltpu.HBM), pl.BlockSpec(memory_space=pl.ANY)],
        out_specs=pl.BlockSpec(memory_space=pltpu.VMEM),
        scratch_shapes=[pltpu.SemaphoreType.DMA((voltages.shape[0],))],
        out_shape=pltpu.VMEM(voltages.shape, voltages.dtype),
        compiler_params=pltpu.CompilerParams(vmem_limit_bytes=VMEM_LIMIT),
    )(pltpu.with_memory_space_constraint(voltages, pltpu.HBM), weights)


def beam_kernel(first_turn, slab_ref, volt_ref, *refs):
    *weight_refs, out_ref, mixed = refs if first_turn == 0 else refs[1:]
    share = weight_refs[0].shape[0]
    _, ports, _, samples = volt_ref.shape
    beams = out_ref.shape[1]
    rows = mixed.shape[1]
    step = pl.program_id(0)

    @pl.when(step == 0)
    def _():
        folded = [ref[c].astype(jnp.float32) for ref in weight_refs for c in range(share)]
        real_rows = stack(*[unfold(f, rows) for f in folded])
        count, size = real_rows.shape
        row, _ = iotas(count, size)
        below, above = pltpu.roll(real_rows, count - 1, 0), pltpu.roll(real_rows, 1, 0)
        imag_rows = jnp.where(row % 2 == 0, -below, above)
        row, col = iotas(size, 2 * ports)
        to_even = (col == 2 * row).astype(jnp.float32).astype(jnp.bfloat16)
        to_odd = (col == 2 * row + 1).astype(jnp.float32).astype(jnp.bfloat16)
        placed = dot_nn(real_rows.astype(jnp.bfloat16), to_even)
        placed = (placed + dot_nn(imag_rows.astype(jnp.bfloat16), to_odd)).astype(jnp.bfloat16)
        for number in range(len(folded)):
            mixed[number] = placed[number * rows : (number + 1) * rows]

    first = (slab_ref[0] ^ (step + first_turn)) * share
    for c in range(share):
        volt = volt_ref[first + c].reshape(2 * ports, samples)
        formed = dot_nn(mixed[step * share + c], volt)
        out_ref[c] = formed[: 2 * beams].astype(jnp.bfloat16).reshape(beams, 2, samples)


def formed_beams(slab, voltages, weights, beams, first_turn=0, formed=None):
    channels, ports, _, samples = voltages.shape
    share = weights[0].shape[0]
    before = [] if formed is None else [formed]
    whole = pl.BlockSpec(weights[0].shape, lambda i, _: (0, 0, 0))
    return pl.pallas_call(
        functools.partial(beam_kernel, first_turn),
        grid_spec=pltpu.PrefetchScalarGridSpec(
            num_scalar_prefetch=1,
            grid=(len(weights),),
            in_specs=[pl.BlockSpec(memory_space=pltpu.VMEM)]
            + [pl.BlockSpec(memory_space=pl.ANY)] * len(before)
            + [whole] * len(weights),
            out_specs=pl.BlockSpec(
                (share, beams, 2, samples), lambda i, slab: (slab[0] ^ (i + first_turn), 0, 0, 0)
            ),
            scratch_shapes=[
                pltpu.VMEM((len(weights) * share, 2 * round_up(beams, 8), 2 * ports), jnp.bfloat16)
            ],
        ),
        out_shape=jax.ShapeDtypeStruct((channels, beams, 2, samples), jnp.bfloat16),
        input_output_aliases={} if formed is None else {2: 0},
        compiler_params=pltpu.CompilerParams(vmem_limit_bytes=VMEM_LIMIT),
    )(slab, voltages, *before, *weights)


def body(voltages, steering, beam_index, channel_flags):
    channel_count, _, port_count, _ = voltages.shape
    beam_count = beam_index.shape[0]
    slabs, blocks = lax.axis_size("slab"), lax.axis_size("chan")
    if channel_count != HW or slabs & (slabs - 1) or not LANES < port_count <= LANES * 3 // 2:
        raise ValueError("unsupported mesh")
    share = channel_count // slabs
    size = LANES + LANES // 2
    half = round_up(beam_count, 8)
    slab = lax.axis_index("slab").astype(jnp.int32).reshape(1)
    first_channel = (lax.axis_index("chan") * channel_count).astype(jnp.int32).reshape(1)
    chosen = chosen_vectors(slab, beam_index, steering, share, half, size)
    by_port = jnp.transpose(voltages, (0, 2, 1, 3))
    across, *inside, own = covariances(first_channel, channel_flags, by_port, size)
    pairs = [[(i, i + 1) for i in range(start, blocks - 1, 2)] for start in range(2)]
    inside_pairs, across_pairs = [ahead + [(j, i) for i, j in ahead] for ahead in pairs]
    across = lax.ppermute(across, "chan", across_pairs)
    inside = jnp.concatenate([lax.ppermute(part, "chan", inside_pairs) for part in inside], axis=0)
    mine, *sent = windows(slab, own, inside, across, slabs)

    def swap(arrays):
        return [
            lax.ppermute(array, "slab", [(i, i ^ turn) for i in range(slabs)])
            for turn, array in enumerate(arrays, 1)
        ]

    got = swap(sent)
    held = held_voltages(by_port, mine)
    first_share = first_channel + slab * share
    weights = solved_weights(first_share, channel_flags, held, mine, got, chosen, port_count, beam_count)
    others = swap([weights] * (slabs - 1))
    beams = formed_beams(slab, held, [weights], beam_count)
    beams = formed_beams(slab, held, others[-1:], beam_count, slabs - 1, beams)
    beams = formed_beams(slab, held, others[:-1], beam_count, 1, beams)
    return jnp.transpose(beams, (0, 2, 1, 3))


def solution(mesh):
    return jax.shard_map(
        body,
        mesh=mesh,
        in_specs=(P("chan", None, None, "slab"), P("chan", None, None, None), P(), P()),
        out_specs=P("chan", None, None, "slab"),
        check_vma=False,
    )
```
